32 devices in a mesh: grp: 2 (over x), wide: 16 (over z, y, core).
Axes of the slice: x: 2, y: 2, z: 4, core: 2. Of those that a mesh axis runs over, the one named last changes fastest.
Arguments:
- voltages: bfloat16 [2048, 2, 8240], P(('grp', 'wide')), parts along dimension 0, may hold values from -6 to 6
- taps: float32 [4, 16], replicated, may hold values from -3 to 3
- flags: int32 [2048], P(('grp', 'wide')), parts along dimension 0, may hold values 0 or 1
- positions: float32 [2, 1024], replicated, may hold values from -20 to 20
- beam_index: int32 [512], P('grp'), parts along dimension 0, may hold values from 0 to 1023
Outputs:
- power: float32 [512, 16, 128], P(('grp', 'wide')), parts along dimension 0
The draws below stay inside these ranges and needn't reach their ends.
There are 2 independent parts, one for each index of `grp`. The reference program is written for one: setup_inputs(seed, part) draws one part's arguments, and reference() takes and returns one part's arrays. A program takes and returns all parts, laid end to end along the dimension named above; an argument that names none is the same for every part. Nothing has to cross between parts.
Inputs may be any that keep to these rules, and one draw needn't show every extreme that they name: 1 keeps an antenna, 0 flags it.
All inputs are finite; a program needn't handle non-finite values. No bound on the sum of `flags` on one device may be relied on, other than what follows from the above.
Results may differ from the reference program's by a relative error of at most 0.0075.
Values may be sent and summed in bfloat16 or wider, within the bound.
A program may use at most 128 MiB of HBM per device.

```python
import math
import jax
import jax.numpy as jnp
from jax import lax

ANTENNAS = 1024
BEAMS = 256
TAPS = 4
ITERS = 2
SPECTRA = 512
CHANNELS = 16


def touch_ends(entries, rng, least, high):
    shape = entries.shape
    index_at = [jax.random.randint(jax.random.fold_in(rng, axis), (), 0, shape[axis]) for axis in range(len(shape))]
    entries = entries.at[tuple(index_at)].set(least)
    longest = shape.index(max(shape))
    index_at[longest] = (index_at[longest] + 1) % shape[longest]
    return entries.at[tuple(index_at)].set(high)


def shard_levels(stream_key, extent, split, low, top_value):
    def one(position, blocks):
        heights = jax.random.uniform(jax.random.fold_in(jax.random.fold_in(stream_key, 6), position), (blocks,), jnp.float32, low / len(split), top_value / len(split))
        return jnp.repeat(jnp.exp(heights), extent[position] // blocks).reshape((-1,) + (1,) * (len(extent) - position - 1))

    gain = one(*split[0])
    for cut in split[1:]:
        gain = gain * one(*cut)
    return gain


def normal_values(key, extent, deviation, bound, shards=(), held_as=jnp.bfloat16):
    values = deviation * jax.random.normal(key, extent, jnp.float32)
    if shards:
        values = values * shard_levels(key, extent, shards, -0.22, 0.18)
    return jnp.clip(values, -bound, bound).astype(held_as)


def setup_inputs(seed: int = 0, part: int = 0) -> dict:
    arg_keys = jax.random.split(jax.random.key(seed), 6)
    part_keys = jax.random.split(jax.random.fold_in(arg_keys[5], part), 6)
    return {
        "voltages": normal_values(part_keys[0], (ANTENNAS, 2, (SPECTRA + TAPS - 1) * CHANNELS), 1.0, 6.0, ((0, 16),)),
        "taps": normal_values(arg_keys[1], (TAPS, CHANNELS), TAPS ** -0.5, 3.0, (), jnp.float32),
        "flags": touch_ends((jax.random.randint(part_keys[2], (ANTENNAS,), 0, 8) < 7).astype(jnp.int32), jax.random.fold_in(part_keys[2], 1), 0, 1),
        "positions": jnp.clip(jax.random.uniform(arg_keys[3], (2, ANTENNAS), jnp.float32, -20.0, 20.0), -20.0, 20.0),
        "beam_index": touch_ends(jax.random.randint(part_keys[4], (BEAMS,), 0, 1024), jax.random.fold_in(part_keys[4], 1), 0, 1023).astype(jnp.int32),
    }


damping = 0.5
grid_side = 32

def channelize(voltages, taps, flags):
    count = voltages.shape[0]
    chans = taps.shape[1]
    ntaps = taps.shape[0]
    total = voltages.shape[2] // chans - ntaps + 1
    samples = voltages.astype(jnp.float32).reshape(count, 2, total + ntaps - 1, chans)
    filtered = taps[0][None, None, None, :] * samples[:, :, 0:total, :]
    for tap in range(1, ntaps):
        filtered = filtered + taps[tap][None, None, None, :] * samples[:, :, tap:tap + total, :]
    branch = jnp.arange(chans, dtype=jnp.int32)
    angle = 2.0 * math.pi / chans * (branch[:, None] * branch[None, :] % chans).astype(jnp.float32)
    cosine = jnp.cos(angle)
    sine = jnp.sin(angle)
    high = lax.Precision.HIGHEST
    real_in = filtered[:, 0]
    imag_in = filtered[:, 1]
    real_out = jnp.einsum('asp,pc->acs', real_in, cosine, precision=high) + jnp.einsum('asp,pc->acs', imag_in, sine, precision=high)
    imag_out = jnp.einsum('asp,pc->acs', imag_in, cosine, precision=high) - jnp.einsum('asp,pc->acs', real_in, sine, precision=high)
    keep = flags.astype(jnp.float32)[:, None, None] / math.sqrt(chans)
    return jnp.stack([real_out * keep, imag_out * keep]).astype(jnp.bfloat16)

def steering(channel, positions, beam_index, chans):
    column = (beam_index % grid_side).astype(jnp.float32)
    row_cell = (beam_index // grid_side).astype(jnp.float32)
    east = (column + 0.5) / grid_side - 0.5
    north = (row_cell + 0.5) / grid_side - 0.5
    ratio = 1.0 + 0.5 * channel.astype(jnp.float32) / chans
    phase = 2.0 * math.pi * ratio * (positions[0][:, None] * east[None, :] + positions[1][:, None] * north[None, :])
    return (jnp.cos(phase), -jnp.sin(phase))

def form_beams(blocks, channel, positions, beam_index, total, chans):
    high = lax.Precision.HIGHEST
    cov_real = 0.0
    cov_imag = 0.0
    for block in blocks:
        left = jnp.concatenate([block[0], block[1]], axis=1)
        turned = jnp.concatenate([block[1], -block[0]], axis=1)
        cov_real = cov_real + jnp.dot(left, left.T, preferred_element_type=jnp.float32)
        cov_imag = cov_imag + jnp.dot(turned, left.T, preferred_element_type=jnp.float32)
    cov_real = cov_real / total
    cov_imag = cov_imag / total
    count = cov_real.shape[0]
    diagonal = jnp.diagonal(cov_real)
    loading = jnp.mean(diagonal) + 1e-05
    scaling = (damping / (diagonal + loading))[:, None]
    steer_real, steer_imag = steering(channel, positions, beam_index, chans)
    weight_real = scaling * steer_real
    weight_imag = scaling * steer_imag
    for sweep in range(ITERS):
        image_real = jnp.dot(cov_real, weight_real, precision=high) - jnp.dot(cov_imag, weight_imag, precision=high) + loading * weight_real
        image_imag = jnp.dot(cov_real, weight_imag, precision=high) + jnp.dot(cov_imag, weight_real, precision=high) + loading * weight_imag
        weight_real = weight_real + scaling * (steer_real - image_real)
        weight_imag = weight_imag + scaling * (steer_imag - image_imag)
    low_real = weight_real.astype(jnp.bfloat16)
    low_imag = weight_imag.astype(jnp.bfloat16)
    plain = jnp.concatenate([low_real, low_imag], axis=0)
    mixed = jnp.concatenate([low_real, -low_imag], axis=0)
    contract = (((0,), (0,)), ((), ()))
    reals = []
    imags = []
    for block in blocks:
        reals.append(lax.dot_general(plain, jnp.concatenate([block[0], block[1]], axis=0), contract, preferred_element_type=jnp.float32))
        imags.append(lax.dot_general(mixed, jnp.concatenate([block[1], block[0]], axis=0), contract, preferred_element_type=jnp.float32))
    norm_factor = 1.0 / math.sqrt(count)
    beams = jnp.stack([jnp.concatenate(reals, axis=-1), jnp.concatenate(imags, axis=-1)]) * norm_factor
    return beams.astype(jnp.bfloat16)

def detect(beams):
    floats = beams.astype(jnp.float32)
    energy = floats[:, 0] * floats[:, 0] + floats[:, 1] * floats[:, 1]
    shape = energy.shape
    return energy.reshape(shape[0], shape[1], shape[2] // 4, 4).sum(axis=-1)

def reference(voltages, taps, flags, positions, beam_index):
    spectra = channelize(voltages, taps, flags)
    chans = taps.shape[1]
    total = spectra.shape[3]
    moved = jnp.moveaxis(spectra, 2, 0)

    def one_channel(operands):
        channel, block = operands
        return form_beams([block], channel, positions, beam_index, total, chans)
    beams = lax.map(one_channel, (jnp.arange(chans, dtype=jnp.int32), moved))
    return jnp.transpose(detect(beams), (1, 0, 2))
```

```python
import functools
import math

import jax
import jax.numpy as jnp
import numpy as np
from jax import lax
from jax.experimental import pallas as pl
from jax.experimental.pallas import tpu as pltpu
from jax.sharding import PartitionSpec as P

ITERS = 2


damping = 0.5
grid_side = 32


def channelize(voltages, taps, flags):
    count = voltages.shape[0]
    chans = taps.shape[1]
    ntaps = taps.shape[0]
    total = voltages.shape[2] // chans - ntaps + 1
    samples = voltages.astype(jnp.float32).reshape(count, 2, total + ntaps - 1, chans)
    filtered = taps[0][None, None, None, :] * samples[:, :, 0:total, :]
    for tap in range(1, ntaps):
        filtered = filtered + taps[tap][None, None, None, :] * samples[:, :, tap : tap + total, :]
    branch = jnp.arange(chans, dtype=jnp.int32)
    angle = 2.0 * math.pi / chans * (branch[:, None] * branch[None, :] % chans).astype(jnp.float32)
    cosine = jnp.cos(angle)
    sine = jnp.sin(angle)
    high = lax.Precision.HIGHEST
    real_in = filtered[:, 0]
    imag_in = filtered[:, 1]
    real_out = jnp.einsum("asp,pc->acs", real_in, cosine, precision=high) + jnp.einsum(
        "asp,pc->acs", imag_in, sine, precision=high
    )
    imag_out = jnp.einsum("asp,pc->acs", imag_in, cosine, precision=high) - jnp.einsum(
        "asp,pc->acs", real_in, sine, precision=high
    )
    keep = flags.astype(jnp.float32)[:, None, None] / math.sqrt(chans)
    return jnp.stack([real_out * keep, imag_out * keep]).astype(jnp.bfloat16)


def steering(channel, positions, beam_index, chans):
    column = (beam_index % grid_side).astype(jnp.float32)
    row_cell = (beam_index // grid_side).astype(jnp.float32)
    east = (column + 0.5) / grid_side - 0.5
    north = (row_cell + 0.5) / grid_side - 0.5
    ratio = 1.0 + 0.5 * channel.astype(jnp.float32) / chans
    phase = (
        2.0
        * math.pi
        * ratio
        * (positions[0][:, None] * east[None, :] + positions[1][:, None] * north[None, :])
    )
    return (jnp.cos(phase), -jnp.sin(phase))


def form_beams(blocks, channel, positions, beam_index, total, chans):
    high = lax.Precision.HIGHEST
    cov_real = 0.0
    cov_imag = 0.0
    for block in blocks:
        left = jnp.concatenate([block[0], block[1]], axis=1)
        turned = jnp.concatenate([block[1], -block[0]], axis=1)
        cov_real = cov_real + jnp.dot(left, left.T, preferred_element_type=jnp.float32)
        cov_imag = cov_imag + jnp.dot(turned, left.T, preferred_element_type=jnp.float32)
    cov_real = cov_real / total
    cov_imag = cov_imag / total
    count = cov_real.shape[0]
    diagonal = jnp.diagonal(cov_real)
    loading = jnp.mean(diagonal) + 1e-05
    scaling = (damping / (diagonal + loading))[:, None]
    steer_real, steer_imag = steering(channel, positions, beam_index, chans)
    weight_real = scaling * steer_real
    weight_imag = scaling * steer_imag
    for sweep in range(ITERS):
        image_real = (
            jnp.dot(cov_real, weight_real, precision=high)
            - jnp.dot(cov_imag, weight_imag, precision=high)
            + loading * weight_real
        )
        image_imag = (
            jnp.dot(cov_real, weight_imag, precision=high)
            + jnp.dot(cov_imag, weight_real, precision=high)
            + loading * weight_imag
        )
        weight_real = weight_real + scaling * (steer_real - image_real)
        weight_imag = weight_imag + scaling * (steer_imag - image_imag)
    low_real = weight_real.astype(jnp.bfloat16)
    low_imag = weight_imag.astype(jnp.bfloat16)
    plain = jnp.concatenate([low_real, low_imag], axis=0)
    mixed = jnp.concatenate([low_real, -low_imag], axis=0)
    contract = (((0,), (0,)), ((), ()))
    reals = []
    imags = []
    for block in blocks:
        reals.append(
            lax.dot_general(
                plain,
                jnp.concatenate([block[0], block[1]], axis=0),
                contract,
                preferred_element_type=jnp.float32,
            )
        )
        imags.append(
            lax.dot_general(
                mixed,
                jnp.concatenate([block[1], block[0]], axis=0),
                contract,
                preferred_element_type=jnp.float32,
            )
        )
    norm_factor = 1.0 / math.sqrt(count)
    beams = (
        jnp.stack([jnp.concatenate(reals, axis=-1), jnp.concatenate(imags, axis=-1)]) * norm_factor
    )
    return beams.astype(jnp.bfloat16)


def detect(beams):
    floats = beams.astype(jnp.float32)
    energy = floats[:, 0] * floats[:, 0] + floats[:, 1] * floats[:, 1]
    shape = energy.shape
    return energy.reshape(shape[0], shape[1], shape[2] // 4, 4).sum(axis=-1)


def plain(voltages, taps, flags, positions, beam_index):
    spectra = channelize(voltages, taps, flags)
    chans = taps.shape[1]
    per_dev = chans // lax.axis_size("wide")
    first = lax.axis_index("wide") * per_dev
    total = spectra.shape[3]
    pieces = [lax.all_to_all(spectra, "wide", split_axis=2, concat_axis=1, tiled=True)]
    stacked = [jnp.moveaxis(piece, 2, 0) for piece in pieces]

    def one_channel(operands):
        offset, blocks = operands
        return form_beams(blocks, first + offset, positions, beam_index, total, chans)

    beams = lax.map(one_channel, (jnp.arange(per_dev, dtype=jnp.int32), stacked))
    result = lax.all_to_all(
        detect(beams).astype(jnp.bfloat16), "wide", split_axis=1, concat_axis=0, tiled=True
    ).astype(jnp.float32)
    return jnp.transpose(result, (1, 0, 2))


MESH = pl.DeviceIdType.MESH
LANES = 128
ROWS = 16
NT = (((1,), (1,)), ((), ()))


def cosine_turns(turns):
    frac = jnp.abs(turns - jnp.floor(turns + 0.5))
    x = (0.25 - frac) * (2.0 * math.pi)
    sq = x * x
    poly = -1.0 / 39916800.0
    for term in (1.0 / 362880.0, -1.0 / 5040.0, 1.0 / 120.0, -1.0 / 6.0, 1.0):
        poly = poly * sq + term
    return x * poly


def swap_halves(block):
    return pltpu.roll(block, LANES // 2, 1)


def kernel(
    volt_ref, order_ref, bank_ref, place_ref, cell_ref, out_ref,
    mixed, sent, spec, steer, weight, low, image, give, got,
    send_sem, recv_sem, own_sem, give_sem, got_sem,
    *, wide, total, chans, window, parts,
):
    me = lax.axis_index("wide")
    peers = wide - 1
    step = total // parts
    beams = cell_ref.shape[0]
    width = wide * LANES

    barrier = pltpu.get_barrier_semaphore()

    def greet(off, carry):
        pl.semaphore_signal(
            barrier, inc=1, device_id={"wide": lax.rem(me + off, wide)}, device_id_type=MESH
        )
        return carry

    lax.fori_loop(1, wide, greet, 0)

    mixed[...] = jnp.dot(
        order_ref[...], volt_ref[...], preferred_element_type=jnp.float32
    ).astype(jnp.bfloat16)

    def spectra_copy(part, other):
        rows = pl.ds(pl.multiple_of(part * step, step), step)
        return pltpu.make_async_remote_copy(
            src_ref=sent.at[other, rows, :],
            dst_ref=spec.at[rows, pl.ds(pl.multiple_of(me * LANES, LANES), LANES)],
            send_sem=send_sem.at[part, other],
            recv_sem=recv_sem.at[part, me],
            device_id={"wide": other},
            device_id_type=MESH,
        )

    def arrival(part, other):
        rows = pl.ds(pl.multiple_of(part * step, step), step)
        return pltpu.make_async_remote_copy(
            src_ref=sent.at[other, rows, :],
            dst_ref=spec.at[rows, pl.ds(pl.multiple_of(other * LANES, LANES), LANES)],
            send_sem=send_sem.at[part, other],
            recv_sem=recv_sem.at[part, other],
            device_id={"wide": other},
            device_id_type=MESH,
        )

    def own_copy(part):
        rows = pl.ds(pl.multiple_of(part * step, step), step)
        return pltpu.make_async_copy(
            sent.at[me, rows, :],
            spec.at[rows, pl.ds(pl.multiple_of(me * LANES, LANES), LANES)],
            own_sem.at[part],
        )

    hop = ROWS * chans
    pairs = step // (2 * ROWS)

    def channelize_pair(pair, carry):
        start = pl.multiple_of(pair * (2 * hop), LANES)
        acc = jnp.zeros((hop, 2 * LANES), jnp.float32)
        for half in range(2):
            rows = slice(half * LANES, (half + 1) * LANES)
            both = jnp.concatenate(
                [
                    mixed[rows, pl.ds(start, window)],
                    mixed[rows, pl.ds(pl.multiple_of(start + hop, LANES), window)],
                ],
                axis=0,
            )
            for piece in range(2):
                acc = acc + lax.dot_general(
                    bank_ref[2 * half + piece], both, NT, preferred_element_type=jnp.float32
                )
        rounded = acc.astype(jnp.bfloat16)
        row = pl.multiple_of(pair * (2 * ROWS), ROWS)
        sent[:, pl.ds(row, ROWS), :] = rounded[:, :LANES].reshape(chans, ROWS, LANES)
        row = pl.multiple_of(row + ROWS, ROWS)
        sent[:, pl.ds(row, ROWS), :] = rounded[:, LANES:].reshape(chans, ROWS, LANES)
        return carry

    for part in range(parts):
        lax.fori_loop(part * pairs, (part + 1) * pairs, channelize_pair, 0)
        if part == 0:
            pl.semaphore_wait(barrier, peers)

        def ship(off, carry, part=part):
            spectra_copy(part, lax.rem(me + off, wide)).start()
            return carry

        lax.fori_loop(1, wide, ship, 0)
        own_copy(part).start()

    ratio = 1.0 + 0.5 * me.astype(jnp.float32) / chans
    east = cell_ref[:, 0:1] * ratio
    north = cell_ref[:, 1:2] * ratio

    def steer_block(block, carry):
        lanes = pl.ds(pl.multiple_of(block * LANES, LANES), LANES)
        turns = east * place_ref[0:1, lanes] + north * place_ref[1:2, lanes]
        steer[:, lanes] = cosine_turns(turns + place_ref[2:3, lanes])
        return carry

    lax.fori_loop(0, wide, steer_block, 0)

    power = jnp.zeros((8, width), jnp.float32)
    for part in range(parts):

        def take(off, carry, part=part):
            arrival(part, lax.rem(me + off, wide)).wait_recv()
            return carry

        lax.fori_loop(1, wide, take, 0)
        own_copy(part).wait()
        for row in range(part * step, (part + 1) * step, ROWS):
            block = spec[row : row + ROWS, :].astype(jnp.float32)
            block = block * block
            power = power + (block[:8] + block[8:])
    power = jnp.sum(power, axis=0, keepdims=True) * (1.0 / total)
    loading = jnp.sum(power) / (width // 2) + 1e-05
    lane = lax.broadcasted_iota(jnp.int32, (1, LANES), 1)
    sign = jnp.where(lane < LANES // 2, 1.0, -1.0)

    scales = []
    for block in range(wide):
        piece = power[:, block * LANES : (block + 1) * LANES]
        piece = piece + swap_halves(jnp.broadcast_to(piece, (8, LANES)))[0:1]
        scales.append(0.5 / (piece + loading))

    def keep_low(lanes, value):
        low[:beams, lanes] = value.astype(jnp.bfloat16)
        low[beams:, lanes] = (swap_halves(value) * sign).astype(jnp.bfloat16)

    for block in range(wide):
        lanes = slice(block * LANES, (block + 1) * LANES)
        value = scales[block] * steer[:, lanes]
        weight[:, lanes] = value
        keep_low(lanes, value)

    half_rows = total // 2

    def project(store):
        for cut in range(2):
            rows = slice(cut * half_rows, (cut + 1) * half_rows)
            store(
                rows,
                lax.dot_general(
                    low[...], spec[rows, :], NT, preferred_element_type=jnp.float32
                ),
            )

    def keep_image(rows, value):
        image[:, rows] = value.astype(jnp.bfloat16)

    for sweep in range(ITERS):
        project(keep_image)
        for duo in range(wide // 2):
            span = slice(2 * duo * LANES, (2 * duo + 2) * LANES)
            back = jnp.dot(image[...], spec[:, span], preferred_element_type=jnp.float32)
            for side in range(2):
                block = 2 * duo + side
                lanes = slice(block * LANES, (block + 1) * LANES)
                cols = slice(side * LANES, (side + 1) * LANES)
                applied = back[:beams, cols] - sign * swap_halves(back[beams:, cols])
                value = weight[:, lanes]
                value = value + scales[block] * (
                    steer[:, lanes] - (applied * (1.0 / total) + loading * value)
                )
                if sweep < ITERS - 1:
                    weight[:, lanes] = value
                keep_low(lanes, value)

    group = total // 4
    share = give.shape[1]
    sums = jnp.zeros((beams, group), jnp.float32)
    for cut in range(2):
        rows = slice(cut * half_rows, (cut + 1) * half_rows)
        value = lax.dot_general(low[...], spec[rows, :], NT, preferred_element_type=jnp.float32)
        energy = value[:beams] * value[:beams] + value[beams:] * value[beams:]
        energy = energy * (2.0 / width)
        top = energy.astype(jnp.bfloat16)
        rest = (energy - top.astype(jnp.float32)).astype(jnp.bfloat16)
        source = lax.broadcasted_iota(jnp.int32, (half_rows, group), 0) + cut * half_rows
        target = lax.broadcasted_iota(jnp.int32, (half_rows, group), 1) * 4
        pick = jnp.where((source >= target) & (source < target + 4), 1.0, 0.0)
        pick = pick.astype(jnp.bfloat16)
        sums = sums + jnp.dot(top, pick, preferred_element_type=jnp.float32)
        sums = sums + jnp.dot(rest, pick, preferred_element_type=jnp.float32)
    give[...] = sums.astype(jnp.bfloat16).reshape(wide, share, group)

    def power_copy(other, slot):
        return pltpu.make_async_remote_copy(
            src_ref=give.at[other],
            dst_ref=got.at[slot],
            send_sem=give_sem.at[other],
            recv_sem=got_sem.at[slot],
            device_id={"wide": other},
            device_id_type=MESH,
        )

    def hand(off, carry):
        power_copy(lax.rem(me + off, wide), me).start()
        return carry

    lax.fori_loop(1, wide, hand, 0)
    mine = pltpu.make_async_copy(give.at[me], got.at[me], own_sem.at[parts])
    mine.start()

    for part in range(parts):

        def settle(off, carry, part=part):
            spectra_copy(part, lax.rem(me + off, wide)).wait_send()
            return carry

        lax.fori_loop(1, wide, settle, 0)

    def close(off, carry):
        other = lax.rem(me + off, wide)
        power_copy(other, other).wait_recv()
        return carry

    lax.fori_loop(1, wide, close, 0)
    mine.wait()
    for channel in range(chans):
        out_ref[:, channel, :] = got[channel].astype(jnp.float32)

    def done(off, carry):
        power_copy(lax.rem(me + off, wide), me).wait_send()
        return carry

    lax.fori_loop(1, wide, done, 0)


def fused(voltages, taps, flags, positions, beam_index):
    wide = lax.axis_size("wide")
    count, _, length = voltages.shape
    ntaps, chans = taps.shape
    total = length // chans - ntaps + 1
    beams = beam_index.shape[0]
    hop = ROWS * chans
    window = -(-(ROWS + ntaps - 1) * chans // LANES) * LANES
    padded = (total // ROWS - 1) * hop + window
    parts = 4
    step = total // parts

    volt = jnp.pad(voltages.reshape(2 * count, length), ((0, 0), (0, padded - length)))

    antenna = np.arange(count)
    base = np.zeros((4 * count, 2 * count), np.float32)
    base[antenna, 2 * antenna] = 1.0
    base[count + antenna, 2 * antenna + 1] = 1.0
    base[2 * count + antenna, 2 * antenna + 1] = 1.0
    base[3 * count + antenna, 2 * antenna] = -1.0
    keep = jnp.repeat(flags.astype(jnp.float32), 2)
    order = (jnp.asarray(base) * keep[None, :]).astype(jnp.bfloat16)

    branch = np.arange(chans)
    angle = 2.0 * math.pi / chans * (branch[:, None] * branch[None, :] % chans)
    waves = (np.stack([np.cos(angle), np.sin(angle)]) / math.sqrt(chans)).astype(np.float32)
    slots = window // chans
    delay = np.arange(slots)[None, :] - np.arange(ROWS)[:, None]
    filt = 0.0
    for tap in range(ntaps):
        here = jnp.asarray((delay == tap).astype(np.float32))
        filt = filt + here[:, :, None] * taps[tap][None, None, :]
    bank = jnp.asarray(waves)[:, :, None, None, :] * filt[None, None]
    bank = bank.reshape(2, hop, window)
    top = bank.astype(jnp.bfloat16)
    rest = (bank - top.astype(jnp.float32)).astype(jnp.bfloat16)
    bank = jnp.stack([top, rest], axis=1).reshape(4, hop, window)

    spread = jnp.broadcast_to(positions.reshape(2, wide, 1, count), (2, wide, 2, count))
    quarter = np.zeros((1, wide, 2, count), np.float32)
    quarter[:, :, 1] = 0.25
    place = jnp.concatenate([spread, jnp.asarray(quarter)]).reshape(3, wide * 2 * count)
    column = (beam_index % grid_side).astype(jnp.float32)
    row_cell = (beam_index // grid_side).astype(jnp.float32)
    cell = jnp.stack(
        [(column + 0.5) / grid_side - 0.5, (row_cell + 0.5) / grid_side - 0.5], axis=1
    )

    share = beams // wide
    width = wide * LANES
    vmem = pl.BlockSpec(memory_space=pltpu.VMEM)
    return pl.pallas_call(
        functools.partial(
            kernel, wide=wide, total=total, chans=chans, window=window, parts=parts
        ),
        out_shape=jax.ShapeDtypeStruct((share, chans, total // 4), jnp.float32),
        in_specs=[vmem] * 5,
        out_specs=vmem,
        scratch_shapes=[
            pltpu.VMEM((2 * LANES, padded), jnp.bfloat16),
            pltpu.VMEM((chans, total, LANES), jnp.bfloat16),
            pltpu.VMEM((total, width), jnp.bfloat16),
            pltpu.VMEM((beams, width), jnp.float32),
            pltpu.VMEM((beams, width), jnp.float32),
            pltpu.VMEM((2 * beams, width), jnp.bfloat16),
            pltpu.VMEM((2 * beams, total), jnp.bfloat16),
            pltpu.VMEM((wide, share, total // 4), jnp.bfloat16),
            pltpu.VMEM((chans, share, total // 4), jnp.bfloat16),
            pltpu.SemaphoreType.DMA((parts, wide)),
            pltpu.SemaphoreType.DMA((parts, wide)),
            pltpu.SemaphoreType.DMA((parts + 1,)),
            pltpu.SemaphoreType.DMA((wide,)),
            pltpu.SemaphoreType.DMA((wide,)),
        ],
        compiler_params=pltpu.CompilerParams(
            collective_id=0, has_side_effects=True, vmem_limit_bytes=48 * 2**20
        ),
    )(volt, order, bank, place, cell)


def fits(voltages, taps, beam_index, wide):
    count, _, length = voltages.shape
    ntaps, chans = taps.shape
    total = length // chans - ntaps + 1
    return (
        2 * count == LANES
        and chans == wide
        and (ROWS * chans) % LANES == 0
        and wide % 2 == 0
        and total % 256 == 0
        and beam_index.shape[0] % (ROWS * wide) == 0
        and (total // 4) % LANES == 0
    )


def local(voltages, taps, flags, positions, beam_index):
    if fits(voltages, taps, beam_index, lax.axis_size("wide")):
        return fused(voltages, taps, flags, positions, beam_index)
    return plain(voltages, taps, flags, positions, beam_index)


def solution(mesh):
    in_specs = (P(("grp", "wide"), None, None), P(), P(("grp", "wide")), P(), P("grp"))
    out_specs = P(("grp", "wide"), None, None)
    return jax.shard_map(local, mesh=mesh, in_specs=in_specs, out_specs=out_specs, check_vma=False)
```

```python
import functools
import math

import jax
import jax.numpy as jnp
import numpy as np
from jax import lax
from jax.experimental import pallas as pl
from jax.experimental.pallas import tpu as pltpu
from jax.sharding import PartitionSpec as P

ITERS = 2


damping = 0.5
grid_side = 32


def channelize(voltages, taps, flags):
    count = voltages.shape[0]
    chans = taps.shape[1]
    ntaps = taps.shape[0]
    total = voltages.shape[2] // chans - ntaps + 1
    samples = voltages.astype(jnp.float32).reshape(count, 2, total + ntaps - 1, chans)
    filtered = taps[0][None, None, None, :] * samples[:, :, 0:total, :]
    for tap in range(1, ntaps):
        filtered = filtered + taps[tap][None, None, None, :] * samples[:, :, tap : tap + total, :]
    branch = jnp.arange(chans, dtype=jnp.int32)
    angle = 2.0 * math.pi / chans * (branch[:, None] * branch[None, :] % chans).astype(jnp.float32)
    cosine = jnp.cos(angle)
    sine = jnp.sin(angle)
    high = lax.Precision.HIGHEST
    real_in = filtered[:, 0]
    imag_in = filtered[:, 1]
    real_out = jnp.einsum("asp,pc->acs", real_in, cosine, precision=high) + jnp.einsum(
        "asp,pc->acs", imag_in, sine, precision=high
    )
    imag_out = jnp.einsum("asp,pc->acs", imag_in, cosine, precision=high) - jnp.einsum(
        "asp,pc->acs", real_in, sine, precision=high
    )
    keep = flags.astype(jnp.float32)[:, None, None] / math.sqrt(chans)
    return jnp.stack([real_out * keep, imag_out * keep]).astype(jnp.bfloat16)


def steering(channel, positions, beam_index, chans):
    column = (beam_index % grid_side).astype(jnp.float32)
    row_cell = (beam_index // grid_side).astype(jnp.float32)
    east = (column + 0.5) / grid_side - 0.5
    north = (row_cell + 0.5) / grid_side - 0.5
    ratio = 1.0 + 0.5 * channel.astype(jnp.float32) / chans
    phase = (
        2.0
        * math.pi
        * ratio
        * (positions[0][:, None] * east[None, :] + positions[1][:, None] * north[None, :])
    )
    return (jnp.cos(phase), -jnp.sin(phase))


def form_beams(blocks, channel, positions, beam_index, total, chans):
    high = lax.Precision.HIGHEST
    cov_real = 0.0
    cov_imag = 0.0
    for block in blocks:
        left = jnp.concatenate([block[0], block[1]], axis=1)
        turned = jnp.concatenate([block[1], -block[0]], axis=1)
        cov_real = cov_real + jnp.dot(left, left.T, preferred_element_type=jnp.float32)
        cov_imag = cov_imag + jnp.dot(turned, left.T, preferred_element_type=jnp.float32)
    cov_real = cov_real / total
    cov_imag = cov_imag / total
    count = cov_real.shape[0]
    diagonal = jnp.diagonal(cov_real)
    loading = jnp.mean(diagonal) + 1e-05
    scaling = (damping / (diagonal + loading))[:, None]
    steer_real, steer_imag = steering(channel, positions, beam_index, chans)
    weight_real = scaling * steer_real
    weight_imag = scaling * steer_imag
    for sweep in range(ITERS):
        image_real = (
            jnp.dot(cov_real, weight_real, precision=high)
            - jnp.dot(cov_imag, weight_imag, precision=high)
            + loading * weight_real
        )
        image_imag = (
            jnp.dot(cov_real, weight_imag, precision=high)
            + jnp.dot(cov_imag, weight_real, precision=high)
            + loading * weight_imag
        )
        weight_real = weight_real + scaling * (steer_real - image_real)
        weight_imag = weight_imag + scaling * (steer_imag - image_imag)
    low_real = weight_real.astype(jnp.bfloat16)
    low_imag = weight_imag.astype(jnp.bfloat16)
    plain = jnp.concatenate([low_real, low_imag], axis=0)
    mixed = jnp.concatenate([low_real, -low_imag], axis=0)
    contract = (((0,), (0,)), ((), ()))
    reals = []
    imags = []
    for block in blocks:
        reals.append(
            lax.dot_general(
                plain,
                jnp.concatenate([block[0], block[1]], axis=0),
                contract,
                preferred_element_type=jnp.float32,
            )
        )
        imags.append(
            lax.dot_general(
                mixed,
                jnp.concatenate([block[1], block[0]], axis=0),
                contract,
                preferred_element_type=jnp.float32,
            )
        )
    norm_factor = 1.0 / math.sqrt(count)
    beams = (
        jnp.stack([jnp.concatenate(reals, axis=-1), jnp.concatenate(imags, axis=-1)]) * norm_factor
    )
    return beams.astype(jnp.bfloat16)


def detect(beams):
    floats = beams.astype(jnp.float32)
    energy = floats[:, 0] * floats[:, 0] + floats[:, 1] * floats[:, 1]
    shape = energy.shape
    return energy.reshape(shape[0], shape[1], shape[2] // 4, 4).sum(axis=-1)


def plain(voltages, taps, flags, positions, beam_index):
    spectra = channelize(voltages, taps, flags)
    chans = taps.shape[1]
    per_dev = chans // lax.axis_size("wide")
    first = lax.axis_index("wide") * per_dev
    total = spectra.shape[3]
    pieces = [lax.all_to_all(spectra, "wide", split_axis=2, concat_axis=1, tiled=True)]
    stacked = [jnp.moveaxis(piece, 2, 0) for piece in pieces]

    def one_channel(operands):
        offset, blocks = operands
        return form_beams(blocks, first + offset, positions, beam_index, total, chans)

    beams = lax.map(one_channel, (jnp.arange(per_dev, dtype=jnp.int32), stacked))
    result = lax.all_to_all(
        detect(beams).astype(jnp.bfloat16), "wide", split_axis=1, concat_axis=0, tiled=True
    ).astype(jnp.float32)
    return jnp.transpose(result, (1, 0, 2))


MESH = pl.DeviceIdType.MESH
LANES = 128
ROWS = 16
NT = (((1,), (1,)), ((), ()))


def cosine_turns(turns):
    frac = jnp.abs(turns - jnp.floor(turns + 0.5))
    x = (0.25 - frac) * (2.0 * math.pi)
    sq = x * x
    poly = -1.0 / 39916800.0
    for term in (1.0 / 362880.0, -1.0 / 5040.0, 1.0 / 120.0, -1.0 / 6.0, 1.0):
        poly = poly * sq + term
    return x * poly


def swap_halves(block):
    return pltpu.roll(block, LANES // 2, 1)


def kernel(
    volt_ref, order_ref, wave_ref, taps_ref, place_ref, cell_ref, out_ref,
    bank, mixed, sent, spec, steer, weight, low, image, applied, scale,
    tell, told, give, got,
    send_sem, recv_sem, own_sem, tell_sem, told_sem, give_sem, got_sem,
    *, wide, total, chans, window, parts,
):
    me = lax.axis_index("wide")
    peers = wide - 1
    step = total // parts
    beams = cell_ref.shape[0]
    width = wide * LANES
    hop = ROWS * chans
    length = volt_ref.shape[2]
    ntaps = taps_ref.shape[0]

    barrier = pltpu.get_barrier_semaphore()

    def everyone(act):
        def body(off, carry):
            act(lax.rem(me + off, wide))
            return carry

        lax.fori_loop(1, wide, body, 0)

    everyone(
        lambda other: pl.semaphore_signal(
            barrier, inc=1, device_id={"wide": other}, device_id_type=MESH
        )
    )

    slot = lax.broadcasted_iota(jnp.int32, (ROWS, window), 1) // chans
    delay = slot - lax.broadcasted_iota(jnp.int32, (ROWS, window), 0)
    filt = jnp.zeros((ROWS, window), jnp.float32)
    for tap in range(ntaps):
        filt = filt + jnp.where(delay == tap, taps_ref[tap : tap + 1, :], 0.0)
    for half in range(2):
        for channel in range(chans):
            rows = slice(channel * ROWS, (channel + 1) * ROWS)
            entry = wave_ref[half, channel : channel + 1, :] * filt
            top = entry.astype(jnp.bfloat16)
            bank[2 * half, rows, :] = top
            bank[2 * half + 1, rows, :] = (entry - top.astype(jnp.float32)).astype(jnp.bfloat16)

    def mix(start, size):
        volt = volt_ref[:, :, start : start + size].reshape(LANES, size)
        mixed[:, start : start + size] = jnp.dot(
            order_ref[...], volt, preferred_element_type=jnp.float32
        ).astype(jnp.bfloat16)

    def rows_of(part):
        return pl.ds(pl.multiple_of(part * step, step), step)

    def lanes_of(block):
        return pl.ds(pl.multiple_of(block * LANES, LANES), LANES)

    def spectra_copy(part, other, owner):
        return pltpu.make_async_remote_copy(
            src_ref=sent.at[other, rows_of(part), :],
            dst_ref=spec.at[rows_of(part), lanes_of(owner)],
            send_sem=send_sem.at[part, other],
            recv_sem=recv_sem.at[part, owner],
            device_id={"wide": other},
            device_id_type=MESH,
        )

    def own_copy(part):
        return pltpu.make_async_copy(
            sent.at[me, rows_of(part), :],
            spec.at[rows_of(part), lanes_of(me)],
            own_sem.at[part],
        )

    def tell_copy(other, owner):
        return pltpu.make_async_remote_copy(
            src_ref=tell.at[other],
            dst_ref=told.at[owner],
            send_sem=tell_sem.at[other],
            recv_sem=told_sem.at[owner],
            device_id={"wide": other},
            device_id_type=MESH,
        )

    pairs = step // (2 * ROWS)
    tell[...] = jnp.zeros_like(tell)

    def channelize_pair(pair, carry):
        start = pl.multiple_of(pair * (2 * hop), LANES)
        acc = jnp.zeros((hop, 2 * LANES), jnp.float32)
        for half in range(2):
            rows = slice(half * LANES, (half + 1) * LANES)
            both = jnp.concatenate(
                [
                    mixed[rows, pl.ds(start, window)],
                    mixed[rows, pl.ds(pl.multiple_of(start + hop, LANES), window)],
                ],
                axis=0,
            )
            for piece in range(2):
                acc = acc + lax.dot_general(
                    bank[2 * half + piece], both, NT, preferred_element_type=jnp.float32
                )
        rounded = acc.astype(jnp.bfloat16)
        for side in range(2):
            row = pl.multiple_of(pair * (2 * ROWS) + side * ROWS, ROWS)
            block = rounded[:, side * LANES : (side + 1) * LANES].reshape(chans, ROWS, LANES)
            sent[:, pl.ds(row, ROWS), :] = block
            block = block.astype(jnp.float32)
            block = block * block
            tell[...] += block[:, :8] + block[:, 8:]
        return carry

    tail = length // LANES * LANES
    mixed[:, tail:] = jnp.zeros((2 * LANES, mixed.shape[1] - tail), jnp.bfloat16)
    over = window - hop
    reach = 0
    for part in range(parts):
        upto = min((part + 1) * step * chans + over, length)
        mix(reach, upto - reach)
        reach = upto
        lax.fori_loop(part * pairs, (part + 1) * pairs, channelize_pair, 0)
        if part == 0:
            pl.semaphore_wait(barrier, peers)
            everyone(lambda other: spectra_copy(0, other, me).start())
            own_copy(0).start()
    everyone(lambda other: tell_copy(other, me).start())
    own_tell = pltpu.make_async_copy(tell.at[me], told.at[me], own_sem.at[parts])
    own_tell.start()
    for part in range(1, parts):
        everyone(lambda other, part=part: spectra_copy(part, other, me).start())
        own_copy(part).start()

    ratio = 1.0 + 0.5 * me.astype(jnp.float32) / chans
    east = cell_ref[:, 0:1] * ratio
    north = cell_ref[:, 1:2] * ratio

    def steer_block(block, carry):
        lanes = lanes_of(block)
        turns = east * place_ref[0:1, lanes] + north * place_ref[1:2, lanes]
        steer[:, lanes] = cosine_turns(turns + place_ref[2:3, lanes])
        return carry

    lax.fori_loop(0, wide, steer_block, 0)

    everyone(lambda other: tell_copy(other, other).wait_recv())
    own_tell.wait()
    lane = lax.broadcasted_iota(jnp.int32, (1, LANES), 1)
    sign = jnp.where(lane < LANES // 2, 1.0, -1.0)
    power = jnp.sum(told[...], axis=1, keepdims=True) * (1.0 / total)
    loading = jnp.sum(power) / (width // 2) + 1e-05
    for block in range(wide):
        piece = jnp.broadcast_to(power[block], (8, LANES))
        piece = piece + swap_halves(piece)
        scale[:, block * LANES : (block + 1) * LANES] = 0.5 / (piece + loading)

    def keep_low(lanes, value):
        low[:beams, lanes] = value.astype(jnp.bfloat16)
        low[beams:, lanes] = (swap_halves(value) * sign).astype(jnp.bfloat16)

    def first_block(block, carry):
        lanes = lanes_of(block)
        value = scale[0:1, lanes] * steer[:, lanes]
        weight[:, lanes] = value
        keep_low(lanes, value)
        return carry

    lax.fori_loop(0, wide, first_block, 0)

    def project(rows):
        return lax.dot_general(low[...], spec[rows, :], NT, preferred_element_type=jnp.float32)

    def back_project(rows, last, sweep, first):
        def duo_block(duo, carry):
            span = pl.ds(pl.multiple_of(duo * (2 * LANES), 2 * LANES), 2 * LANES)
            back = jnp.dot(image[:, rows], spec[rows, span], preferred_element_type=jnp.float32)
            for side in range(2):
                lanes = lanes_of(2 * duo + side)
                cols = slice(side * LANES, (side + 1) * LANES)
                fresh = back[:beams, cols] - sign * swap_halves(back[beams:, cols])
                if not first:
                    fresh = applied[:, lanes] + fresh
                if not last:
                    applied[:, lanes] = fresh
                    continue
                value = weight[:, lanes]
                value = value + scale[0:1, lanes] * (
                    steer[:, lanes] - (fresh * (1.0 / total) + loading * value)
                )
                if sweep < ITERS - 1:
                    weight[:, lanes] = value
                keep_low(lanes, value)
            return carry

        lax.fori_loop(0, wide // 2, duo_block, 0)

    groups = [(0, 2), (2, 3), (3, 4)]
    for begin, end in groups:
        for part in range(begin, end):
            everyone(lambda other, part=part: spectra_copy(part, other, other).wait_recv())
            own_copy(part).wait()
        rows = slice(begin * step, end * step)
        image[:, rows] = project(rows).astype(jnp.bfloat16)
        back_project(rows, end == parts, 0, begin == 0)

    half_rows = total // 2
    halves = [slice(cut * half_rows, (cut + 1) * half_rows) for cut in range(2)]
    for sweep in range(1, ITERS):
        for rows in halves:
            image[:, rows] = project(rows).astype(jnp.bfloat16)
        back_project(slice(0, total), True, sweep, True)

    group = total // 4
    share = give.shape[1]
    sums = jnp.zeros((beams, group), jnp.float32)
    for cut, rows in enumerate(halves):
        value = project(rows)
        energy = value[:beams] * value[:beams] + value[beams:] * value[beams:]
        energy = energy * (2.0 / width)
        top = energy.astype(jnp.bfloat16)
        rest = (energy - top.astype(jnp.float32)).astype(jnp.bfloat16)
        source = lax.broadcasted_iota(jnp.int32, (half_rows, group), 0) + cut * half_rows
        target = lax.broadcasted_iota(jnp.int32, (half_rows, group), 1) * 4
        pick = jnp.where((source >= target) & (source < target + 4), 1.0, 0.0)
        pick = pick.astype(jnp.bfloat16)
        sums = sums + jnp.dot(top, pick, preferred_element_type=jnp.float32)
        sums = sums + jnp.dot(rest, pick, preferred_element_type=jnp.float32)
    give[...] = sums.astype(jnp.bfloat16).reshape(wide, share, group)

    def power_copy(other, owner):
        return pltpu.make_async_remote_copy(
            src_ref=give.at[other],
            dst_ref=got.at[owner],
            send_sem=give_sem.at[other],
            recv_sem=got_sem.at[owner],
            device_id={"wide": other},
            device_id_type=MESH,
        )

    everyone(lambda other: power_copy(other, me).start())
    mine = pltpu.make_async_copy(give.at[me], got.at[me], own_sem.at[parts + 1])
    mine.start()
    for part in range(parts):
        everyone(lambda other, part=part: spectra_copy(part, other, me).wait_send())
    everyone(lambda other: tell_copy(other, me).wait_send())
    everyone(lambda other: power_copy(other, other).wait_recv())
    mine.wait()
    for channel in range(chans):
        out_ref[:, channel, :] = got[channel].astype(jnp.float32)
    everyone(lambda other: power_copy(other, me).wait_send())


def fused(voltages, taps, flags, positions, beam_index):
    wide = lax.axis_size("wide")
    count, _, length = voltages.shape
    ntaps, chans = taps.shape
    total = length // chans - ntaps + 1
    beams = beam_index.shape[0]
    hop = ROWS * chans
    window = -(-(ROWS + ntaps - 1) * chans // LANES) * LANES
    padded = (total // ROWS - 1) * hop + window
    parts = 4

    antenna = np.arange(count)
    base = np.zeros((4 * count, 2 * count), np.float32)
    base[antenna, 2 * antenna] = 1.0
    base[count + antenna, 2 * antenna + 1] = 1.0
    base[2 * count + antenna, 2 * antenna + 1] = 1.0
    base[3 * count + antenna, 2 * antenna] = -1.0
    keep = jnp.repeat(flags.astype(jnp.float32), 2)
    order = (jnp.asarray(base) * keep[None, :]).astype(jnp.bfloat16)

    branch = np.arange(chans)
    angle = 2.0 * math.pi / chans * (branch[:, None] * branch[None, :] % chans)
    waves = np.stack([np.cos(angle), np.sin(angle)]).swapaxes(1, 2) / math.sqrt(chans)
    waves = np.tile(waves.astype(np.float32), (1, 1, window // chans))
    tiled = jnp.tile(taps, (1, window // chans))

    spread = jnp.broadcast_to(positions.reshape(2, wide, 1, count), (2, wide, 2, count))
    quarter = np.zeros((1, wide, 2, count), np.float32)
    quarter[:, :, 1] = 0.25
    place = jnp.concatenate([spread, jnp.asarray(quarter)]).reshape(3, wide * 2 * count)
    column = (beam_index % grid_side).astype(jnp.float32)
    row_cell = (beam_index // grid_side).astype(jnp.float32)
    cell = jnp.stack(
        [(column + 0.5) / grid_side - 0.5, (row_cell + 0.5) / grid_side - 0.5], axis=1
    )

    share = beams // wide
    width = wide * LANES
    vmem = pl.BlockSpec(memory_space=pltpu.VMEM)
    return pl.pallas_call(
        functools.partial(
            kernel, wide=wide, total=total, chans=chans, window=window, parts=parts
        ),
        out_shape=jax.ShapeDtypeStruct((share, chans, total // 4), jnp.float32),
        in_specs=[vmem] * 6,
        out_specs=vmem,
        scratch_shapes=[
            pltpu.VMEM((4, hop, window), jnp.bfloat16),
            pltpu.VMEM((2 * LANES, padded), jnp.bfloat16),
            pltpu.VMEM((chans, total, LANES), jnp.bfloat16),
            pltpu.VMEM((total, width), jnp.bfloat16),
            pltpu.VMEM((beams, width), jnp.float32),
            pltpu.VMEM((beams, width), jnp.float32),
            pltpu.VMEM((2 * beams, width), jnp.bfloat16),
            pltpu.VMEM((2 * beams, total), jnp.bfloat16),
            pltpu.VMEM((beams, width), jnp.float32),
            pltpu.VMEM((8, width), jnp.float32),
            pltpu.VMEM((chans, 8, LANES), jnp.float32),
            pltpu.VMEM((wide, 8, LANES), jnp.float32),
            pltpu.VMEM((wide, share, total // 4), jnp.bfloat16),
            pltpu.VMEM((chans, share, total // 4), jnp.bfloat16),
            pltpu.SemaphoreType.DMA((parts, wide)),
            pltpu.SemaphoreType.DMA((parts, wide)),
            pltpu.SemaphoreType.DMA((parts + 2,)),
            pltpu.SemaphoreType.DMA((wide,)),
            pltpu.SemaphoreType.DMA((wide,)),
            pltpu.SemaphoreType.DMA((wide,)),
            pltpu.SemaphoreType.DMA((wide,)),
        ],
        compiler_params=pltpu.CompilerParams(
            collective_id=0, has_side_effects=True, vmem_limit_bytes=48 * 2**20
        ),
    )(voltages, order, jnp.asarray(waves), tiled, place, cell)


def fits(voltages, taps, beam_index, wide):
    count, _, length = voltages.shape
    ntaps, chans = taps.shape
    total = length // chans - ntaps + 1
    return (
        2 * count == LANES
        and chans == wide
        and (ROWS * chans) % LANES == 0
        and wide % 2 == 0
        and total % 256 == 0
        and beam_index.shape[0] % (ROWS * wide) == 0
        and (total // 4) % LANES == 0
    )


def local(voltages, taps, flags, positions, beam_index):
    if fits(voltages, taps, beam_index, lax.axis_size("wide")):
        return fused(voltages, taps, flags, positions, beam_index)
    return plain(voltages, taps, flags, positions, beam_index)


def solution(mesh):
    in_specs = (P(("grp", "wide"), None, None), P(), P(("grp", "wide")), P(), P("grp"))
    out_specs = P(("grp", "wide"), None, None)
    return jax.shard_map(local, mesh=mesh, in_specs=in_specs, out_specs=out_specs, check_vma=False)
```

```python
import functools
import math

import jax
import jax.numpy as jnp
import numpy as np
from jax import lax
from jax.experimental import pallas as pl
from jax.experimental.pallas import tpu as pltpu
from jax.sharding import PartitionSpec as P

ITERS = 2


damping = 0.5
grid_side = 32


def channelize(voltages, taps, flags):
    count = voltages.shape[0]
    chans = taps.shape[1]
    ntaps = taps.shape[0]
    total = voltages.shape[2] // chans - ntaps + 1
    samples = voltages.astype(jnp.float32).reshape(count, 2, total + ntaps - 1, chans)
    filtered = taps[0][None, None, None, :] * samples[:, :, 0:total, :]
    for tap in range(1, ntaps):
        filtered = filtered + taps[tap][None, None, None, :] * samples[:, :, tap : tap + total, :]
    branch = jnp.arange(chans, dtype=jnp.int32)
    angle = 2.0 * math.pi / chans * (branch[:, None] * branch[None, :] % chans).astype(jnp.float32)
    cosine = jnp.cos(angle)
    sine = jnp.sin(angle)
    high = lax.Precision.HIGHEST
    real_in = filtered[:, 0]
    imag_in = filtered[:, 1]
    real_out = jnp.einsum("asp,pc->acs", real_in, cosine, precision=high) + jnp.einsum(
        "asp,pc->acs", imag_in, sine, precision=high
    )
    imag_out = jnp.einsum("asp,pc->acs", imag_in, cosine, precision=high) - jnp.einsum(
        "asp,pc->acs", real_in, sine, precision=high
    )
    keep = flags.astype(jnp.float32)[:, None, None] / math.sqrt(chans)
    return jnp.stack([real_out * keep, imag_out * keep]).astype(jnp.bfloat16)


def steering(channel, positions, beam_index, chans):
    column = (beam_index % grid_side).astype(jnp.float32)
    row_cell = (beam_index // grid_side).astype(jnp.float32)
    east = (column + 0.5) / grid_side - 0.5
    north = (row_cell + 0.5) / grid_side - 0.5
    ratio = 1.0 + 0.5 * channel.astype(jnp.float32) / chans
    phase = (
        2.0
        * math.pi
        * ratio
        * (positions[0][:, None] * east[None, :] + positions[1][:, None] * north[None, :])
    )
    return (jnp.cos(phase), -jnp.sin(phase))


def form_beams(blocks, channel, positions, beam_index, total, chans):
    high = lax.Precision.HIGHEST
    cov_real = 0.0
    cov_imag = 0.0
    for block in blocks:
        left = jnp.concatenate([block[0], block[1]], axis=1)
        turned = jnp.concatenate([block[1], -block[0]], axis=1)
        cov_real = cov_real + jnp.dot(left, left.T, preferred_element_type=jnp.float32)
        cov_imag = cov_imag + jnp.dot(turned, left.T, preferred_element_type=jnp.float32)
    cov_real = cov_real / total
    cov_imag = cov_imag / total
    count = cov_real.shape[0]
    diagonal = jnp.diagonal(cov_real)
    loading = jnp.mean(diagonal) + 1e-05
    scaling = (damping / (diagonal + loading))[:, None]
    steer_real, steer_imag = steering(channel, positions, beam_index, chans)
    weight_real = scaling * steer_real
    weight_imag = scaling * steer_imag
    for sweep in range(ITERS):
        image_real = (
            jnp.dot(cov_real, weight_real, precision=high)
            - jnp.dot(cov_imag, weight_imag, precision=high)
            + loading * weight_real
        )
        image_imag = (
            jnp.dot(cov_real, weight_imag, precision=high)
            + jnp.dot(cov_imag, weight_real, precision=high)
            + loading * weight_imag
        )
        weight_real = weight_real + scaling * (steer_real - image_real)
        weight_imag = weight_imag + scaling * (steer_imag - image_imag)
    low_real = weight_real.astype(jnp.bfloat16)
    low_imag = weight_imag.astype(jnp.bfloat16)
    plain = jnp.concatenate([low_real, low_imag], axis=0)
    mixed = jnp.concatenate([low_real, -low_imag], axis=0)
    contract = (((0,), (0,)), ((), ()))
    reals = []
    imags = []
    for block in blocks:
        reals.append(
            lax.dot_general(
                plain,
                jnp.concatenate([block[0], block[1]], axis=0),
                contract,
                preferred_element_type=jnp.float32,
            )
        )
        imags.append(
            lax.dot_general(
                mixed,
                jnp.concatenate([block[1], block[0]], axis=0),
                contract,
                preferred_element_type=jnp.float32,
            )
        )
    norm_factor = 1.0 / math.sqrt(count)
    beams = (
        jnp.stack([jnp.concatenate(reals, axis=-1), jnp.concatenate(imags, axis=-1)]) * norm_factor
    )
    return beams.astype(jnp.bfloat16)


def detect(beams):
    floats = beams.astype(jnp.float32)
    energy = floats[:, 0] * floats[:, 0] + floats[:, 1] * floats[:, 1]
    shape = energy.shape
    return energy.reshape(shape[0], shape[1], shape[2] // 4, 4).sum(axis=-1)


def plain(voltages, taps, flags, positions, beam_index):
    spectra = channelize(voltages, taps, flags)
    chans = taps.shape[1]
    per_dev = chans // lax.axis_size("wide")
    first = lax.axis_index("wide") * per_dev
    total = spectra.shape[3]
    pieces = [lax.all_to_all(spectra, "wide", split_axis=2, concat_axis=1, tiled=True)]
    stacked = [jnp.moveaxis(piece, 2, 0) for piece in pieces]

    def one_channel(operands):
        offset, blocks = operands
        return form_beams(blocks, first + offset, positions, beam_index, total, chans)

    beams = lax.map(one_channel, (jnp.arange(per_dev, dtype=jnp.int32), stacked))
    result = lax.all_to_all(
        detect(beams).astype(jnp.bfloat16), "wide", split_axis=1, concat_axis=0, tiled=True
    ).astype(jnp.float32)
    return jnp.transpose(result, (1, 0, 2))


MESH = pl.DeviceIdType.MESH
LANES = 128
ROWS = 16
NT = (((1,), (1,)), ((), ()))


def cosine_turns(turns):
    frac = jnp.abs(turns - jnp.floor(turns + 0.5))
    x = (0.25 - frac) * (2.0 * math.pi)
    sq = x * x
    poly = -1.0 / 39916800.0
    for term in (1.0 / 362880.0, -1.0 / 5040.0, 1.0 / 120.0, -1.0 / 6.0, 1.0):
        poly = poly * sq + term
    return x * poly


def swap_halves(block):
    return pltpu.roll(block, LANES // 2, 1)


def kernel(
    volt_hbm, taps_ref, flags_ref, place_ref, index_ref, out_ref,
    volt, bank, mixed, sent, spec, steer, weight, low, image, applied, scale,
    tell, told, give, got,
    volt_sem, send_sem, recv_sem, tell_sem, told_sem, give_sem, got_sem,
    *, wide, total, chans, window, bounds, early,
):
    me = lax.axis_index("wide")
    parts = len(bounds) - 1
    beams = index_ref.shape[1]
    width = wide * LANES
    hop = ROWS * chans
    length = volt_hbm.shape[2]
    ntaps = taps_ref.shape[0]
    half_lanes = LANES // 2

    barrier = pltpu.get_barrier_semaphore()
    fetch = pltpu.make_async_copy(volt_hbm, volt, volt_sem.at[0])
    fetch.start()

    def greet(off, carry):
        pl.semaphore_signal(
            barrier, inc=1, device_id={"wide": lax.rem(me + off, wide)}, device_id_type=MESH
        )
        return carry

    lax.fori_loop(1, wide, greet, 0)

    ranked = sorted(range(1, wide), key=lambda off: (abs(off - wide // 2), off))
    cut = (len(ranked) + 1) // 2
    mixed_order = [
        entry for duo in zip(ranked[:cut], ranked[cut:] + [None]) for entry in duo
    ]
    mixed_order = [entry for entry in mixed_order if entry is not None]
    turned_order = list(mixed_order)
    for at in range(0, len(turned_order) - 1, 2):
        turned_order[at], turned_order[at + 1] = turned_order[at + 1], turned_order[at]

    def everyone(act):
        core = lax.rem(me, 2)
        for one, two in zip(mixed_order, turned_order):
            act(lax.rem(me + (one + core * (two - one)), wide))

    def iota(shape, axis):
        return lax.broadcasted_iota(jnp.int32, shape, axis)

    slot = iota((ROWS, window), 1) // chans
    delay = slot - iota((ROWS, window), 0)
    spread = jnp.where(iota((chans, window), 1) % chans == iota((chans, window), 0), 1.0, 0.0)
    tiled = jnp.dot(
        taps_ref[...], spread, precision=lax.Precision.HIGHEST, preferred_element_type=jnp.float32
    )
    filt = jnp.zeros((ROWS, window), jnp.float32)
    for tap in range(ntaps):
        filt = filt + jnp.where(delay == tap, tiled[tap : tap + 1, :], 0.0)
    spin = (iota((chans, window), 0) * (iota((chans, window), 1) % chans)) % chans
    spin = spin.astype(jnp.float32) / chans
    for half in range(2):
        wave = cosine_turns(spin - 0.25 * half) / math.sqrt(chans)
        for channel in range(chans):
            entry = wave[channel : channel + 1, :] * filt
            top = entry.astype(jnp.bfloat16)
            rest = (entry - top.astype(jnp.float32)).astype(jnp.bfloat16)
            bank[half, channel * ROWS : (channel + 1) * ROWS, :] = top
            bank[half, hop + channel * ROWS : hop + (channel + 1) * ROWS, :] = rest

    doubled = jnp.where(iota((half_lanes, LANES), 1) // 2 == iota((half_lanes, LANES), 0), 1.0, 0.0)
    keep = jnp.broadcast_to(flags_ref[...].astype(jnp.float32), (8, half_lanes))
    keep = jnp.dot(
        keep.astype(jnp.bfloat16), doubled.astype(jnp.bfloat16), preferred_element_type=jnp.float32
    )[0:1]
    row = iota((2 * LANES, LANES), 0)
    antenna = row % half_lanes
    quarter = row // half_lanes
    from_part = jnp.where((quarter == 1) | (quarter == 2), 1, 0)
    chosen = iota((2 * LANES, LANES), 1) == 2 * antenna + from_part
    order = jnp.where(chosen, jnp.where(quarter == 3, -keep, keep), 0.0).astype(jnp.bfloat16)

    def mix(start, size):
        block = volt[:, :, start : start + size].reshape(LANES, size)
        mixed[:, start : start + size] = jnp.dot(
            order, block, preferred_element_type=jnp.float32
        ).astype(jnp.bfloat16)

    def rows_of(part):
        return slice(bounds[part], bounds[part + 1])

    def lanes_of(block):
        return pl.ds(pl.multiple_of(block * LANES, LANES), LANES)

    def remote(source, target, out_sem, in_sem, other):
        return pltpu.make_async_remote_copy(
            src_ref=source,
            dst_ref=target,
            send_sem=out_sem,
            recv_sem=in_sem,
            device_id={"wide": other},
            device_id_type=MESH,
        )

    def await_bytes(ref, sem):
        pltpu.make_async_copy(ref, ref, sem).wait()

    def ship(part):
        rows = rows_of(part)
        everyone(
            lambda other: remote(
                sent.at[other, rows, :], spec.at[me, rows, :],
                send_sem.at[part], recv_sem.at[part], other,
            ).start()
        )
        pltpu.make_async_copy(
            sent.at[me, rows, :], spec.at[me, rows, :], recv_sem.at[part]
        ).start()

    tell[...] = jnp.zeros_like(tell)

    def channelize_pair(pair, carry):
        start = pl.multiple_of(pair * (2 * hop), LANES)
        acc = jnp.zeros((2 * hop, 2 * LANES), jnp.float32)
        for half in range(2):
            rows = slice(half * LANES, (half + 1) * LANES)
            both = jnp.concatenate(
                [
                    mixed[rows, pl.ds(start, window)],
                    mixed[rows, pl.ds(pl.multiple_of(start + hop, LANES), window)],
                ],
                axis=0,
            )
            acc = acc + lax.dot_general(
                bank[half], both, NT, preferred_element_type=jnp.float32
            )
        rounded = (acc[:hop] + acc[hop:]).astype(jnp.bfloat16)
        for side in range(2):
            at = pl.multiple_of(pair * (2 * ROWS) + side * ROWS, ROWS)
            block = rounded[:, side * LANES : (side + 1) * LANES].reshape(chans, ROWS, LANES)
            sent[:, pl.ds(at, ROWS), :] = block
            block = block.astype(jnp.float32)
            block = block * block
            tell[...] += block[:, :8] + block[:, 8:]
        return carry

    fetch.wait()
    tail = length // LANES * LANES
    mixed[:, tail:] = jnp.zeros((2 * LANES, mixed.shape[1] - tail), jnp.bfloat16)
    over = window - hop
    reach = 0
    for part in range(parts):
        upto = min(bounds[part + 1] * chans + over, length)
        mix(reach, upto - reach)
        reach = upto
        span = 2 * ROWS
        lax.fori_loop(bounds[part] // span, bounds[part + 1] // span, channelize_pair, 0)
        if part == 0:
            pl.semaphore_wait(barrier, wide - 1)
        if part < early:
            ship(part)
    everyone(
        lambda other: remote(
            tell.at[other], told.at[me], tell_sem.at[0], told_sem.at[0], other
        ).start()
    )
    pltpu.make_async_copy(tell.at[me], told.at[me], told_sem.at[0]).start()
    for part in range(early, parts):
        ship(part)

    index = index_ref[...]
    ratio = 1.0 + 0.5 * me.astype(jnp.float32) / chans
    cells = [
        ((index % grid_side).astype(jnp.float32) + 0.5) / grid_side - 0.5,
        ((index // grid_side).astype(jnp.float32) + 0.5) / grid_side - 0.5,
    ]
    same = iota((beams, beams), 0) == iota((beams, beams), 1)
    east, north = [
        jnp.sum(jnp.where(same, cell, 0.0), axis=1, keepdims=True) * ratio for cell in cells
    ]
    first_half = iota((1, LANES), 1) < half_lanes
    turn = jnp.where(first_half, 0.0, 0.25)

    def steer_duo(duo, carry):
        here = place_ref[:, lanes_of(duo)]
        here = jnp.concatenate([here, jnp.zeros((6, LANES), jnp.float32)], axis=0)
        there = swap_halves(here)
        for side in range(2):
            both = jnp.where(first_half, here, there) if side == 0 else jnp.where(
                first_half, there, here
            )
            turns = east * both[0:1] + north * both[1:2] + turn
            steer[:, lanes_of(2 * duo + side)] = cosine_turns(turns)
        return carry

    lax.fori_loop(0, wide // 2, steer_duo, 0)

    await_bytes(told, told_sem.at[0])
    sign = jnp.where(first_half, 1.0, -1.0)
    power = jnp.sum(told[...], axis=1, keepdims=True) * (1.0 / total)
    loading = jnp.sum(power) / (width // 2) + 1e-05
    for block in range(wide):
        piece = jnp.broadcast_to(power[block], (8, LANES))
        piece = piece + swap_halves(piece)
        scale[:, block * LANES : (block + 1) * LANES] = 0.5 / (piece + loading)

    def keep_low(lanes, value):
        low[:beams, lanes] = value.astype(jnp.bfloat16)
        low[beams:, lanes] = (swap_halves(value) * sign).astype(jnp.bfloat16)

    def first_block(block, carry):
        lanes = lanes_of(block)
        value = scale[0:1, lanes] * steer[:, lanes]
        weight[:, lanes] = value
        keep_low(lanes, value)
        return carry

    lax.fori_loop(0, wide, first_block, 0)

    def project(rows):
        strip = jnp.concatenate([spec[block, rows, :] for block in range(wide)], axis=1)
        return lax.dot_general(low[...], strip, NT, preferred_element_type=jnp.float32)

    def back_project(rows, last, sweep, first):
        def duo_block(duo, carry):
            strip = jnp.concatenate([spec[2 * duo, rows, :], spec[2 * duo + 1, rows, :]], axis=1)
            back = jnp.dot(image[:, rows], strip, preferred_element_type=jnp.float32)
            for side in range(2):
                lanes = lanes_of(2 * duo + side)
                cols = slice(side * LANES, (side + 1) * LANES)
                fresh = back[:beams, cols] - sign * swap_halves(back[beams:, cols])
                if not first:
                    fresh = applied[:, lanes] + fresh
                if not last:
                    applied[:, lanes] = fresh
                    continue
                value = weight[:, lanes]
                value = value + scale[0:1, lanes] * (
                    steer[:, lanes] - (fresh * (1.0 / total) + loading * value)
                )
                if sweep < ITERS - 1:
                    weight[:, lanes] = value
                keep_low(lanes, value)
            return carry

        lax.fori_loop(0, wide // 2, duo_block, 0)

    for part in range(parts):
        rows = rows_of(part)
        await_bytes(spec.at[:, rows, :], recv_sem.at[part])
        if bounds[part + 1] % LANES and part + 1 < parts:
            continue
        rows = slice(bounds[part] // LANES * LANES, bounds[part + 1])
        image[:, rows] = project(rows).astype(jnp.bfloat16)
        back_project(rows, part + 1 == parts, 0, rows.start == 0)

    half_rows = total // 2
    halves = [slice(half * half_rows, (half + 1) * half_rows) for half in range(2)]
    for sweep in range(1, ITERS):
        for rows in halves:
            image[:, rows] = project(rows).astype(jnp.bfloat16)
        back_project(slice(0, total), True, sweep, True)

    group = total // 4
    share = give.shape[1]
    sums = jnp.zeros((beams, group), jnp.float32)
    for half, rows in enumerate(halves):
        value = project(rows)
        energy = value[:beams] * value[:beams] + value[beams:] * value[beams:]
        energy = energy * (2.0 / width)
        top = energy.astype(jnp.bfloat16)
        rest = (energy - top.astype(jnp.float32)).astype(jnp.bfloat16)
        source = iota((half_rows, group), 0) + half * half_rows
        target = iota((half_rows, group), 1) * 4
        pick = jnp.where((source >= target) & (source < target + 4), 1.0, 0.0)
        pick = pick.astype(jnp.bfloat16)
        sums = sums + jnp.dot(top, pick, preferred_element_type=jnp.float32)
        sums = sums + jnp.dot(rest, pick, preferred_element_type=jnp.float32)
    give[...] = sums.astype(jnp.bfloat16).reshape(wide, share, group)
    everyone(
        lambda other: remote(
            give.at[other], got.at[me], give_sem.at[0], got_sem.at[0], other
        ).start()
    )
    pltpu.make_async_copy(give.at[me], got.at[me], got_sem.at[0]).start()
    for part in range(parts):
        await_bytes(sent.at[: wide - 1, rows_of(part), :], send_sem.at[part])
    await_bytes(tell.at[: wide - 1], tell_sem.at[0])
    await_bytes(got, got_sem.at[0])
    for channel in range(chans):
        out_ref[:, channel, :] = got[channel].astype(jnp.float32)
    await_bytes(give.at[: wide - 1], give_sem.at[0])


def fused(voltages, taps, flags, positions, beam_index):
    wide = lax.axis_size("wide")
    count, _, length = voltages.shape
    ntaps, chans = taps.shape
    total = length // chans - ntaps + 1
    beams = beam_index.shape[0]
    hop = ROWS * chans
    window = -(-(ROWS + ntaps - 1) * chans // LANES) * LANES
    padded = (total // ROWS - 1) * hop + window
    bounds = [0, LANES // 2] + list(range(LANES, total + 1, LANES))
    parts = len(bounds) - 1
    share = beams // wide
    width = wide * LANES
    vmem = pl.BlockSpec(memory_space=pltpu.VMEM)
    return pl.pallas_call(
        functools.partial(
            kernel, wide=wide, total=total, chans=chans, window=window, bounds=bounds,
            early=min(3, parts),
        ),
        out_shape=jax.ShapeDtypeStruct((share, chans, total // 4), jnp.float32),
        in_specs=[pl.BlockSpec(memory_space=pl.ANY)] + [vmem] * 4,
        out_specs=vmem,
        scratch_shapes=[
            pltpu.VMEM(voltages.shape, jnp.bfloat16),
            pltpu.VMEM((2, 2 * hop, window), jnp.bfloat16),
            pltpu.VMEM((2 * LANES, padded), jnp.bfloat16),
            pltpu.VMEM((chans, total, LANES), jnp.bfloat16),
            pltpu.VMEM((wide, total, LANES), jnp.bfloat16),
            pltpu.VMEM((beams, width), jnp.float32),
            pltpu.VMEM((beams, width), jnp.float32),
            pltpu.VMEM((2 * beams, width), jnp.bfloat16),
            pltpu.VMEM((2 * beams, total), jnp.bfloat16),
            pltpu.VMEM((beams, width), jnp.float32),
            pltpu.VMEM((8, width), jnp.float32),
            pltpu.VMEM((chans, 8, LANES), jnp.float32),
            pltpu.VMEM((wide, 8, LANES), jnp.float32),
            pltpu.VMEM((wide, share, total // 4), jnp.bfloat16),
            pltpu.VMEM((chans, share, total // 4), jnp.bfloat16),
            pltpu.SemaphoreType.DMA((1,)),
            pltpu.SemaphoreType.DMA((parts,)),
            pltpu.SemaphoreType.DMA((parts,)),
            pltpu.SemaphoreType.DMA((1,)),
            pltpu.SemaphoreType.DMA((1,)),
            pltpu.SemaphoreType.DMA((1,)),
            pltpu.SemaphoreType.DMA((1,)),
        ],
        compiler_params=pltpu.CompilerParams(
            collective_id=0, has_side_effects=True, vmem_limit_bytes=52 * 2**20
        ),
    )(voltages, taps, flags.reshape(1, -1), positions, beam_index.reshape(1, -1))


def fits(voltages, taps, beam_index, wide):
    count, _, length = voltages.shape
    ntaps, chans = taps.shape
    total = length // chans - ntaps + 1
    return (
        2 * count == LANES
        and chans == wide
        and (ROWS * chans) % LANES == 0
        and wide % 2 == 0
        and total % 256 == 0
        and beam_index.shape[0] % (ROWS * wide) == 0
        and (total // 4) % LANES == 0
    )


def local(voltages, taps, flags, positions, beam_index):
    if fits(voltages, taps, beam_index, lax.axis_size("wide")):
        return fused(voltages, taps, flags, positions, beam_index)
    return plain(voltages, taps, flags, positions, beam_index)


def solution(mesh):
    in_specs = (P(("grp", "wide"), None, None), P(), P(("grp", "wide")), P(), P("grp"))
    out_specs = P(("grp", "wide"), None, None)
    return jax.shard_map(local, mesh=mesh, in_specs=in_specs, out_specs=out_specs, check_vma=False)
```

```python
import functools
import math

import jax
import jax.numpy as jnp
import numpy as np
from jax import lax
from jax.experimental import pallas as pl
from jax.experimental.pallas import tpu as pltpu
from jax.sharding import PartitionSpec as P

ITERS = 2


damping = 0.5
grid_side = 32


def channelize(voltages, taps, flags):
    count = voltages.shape[0]
    chans = taps.shape[1]
    ntaps = taps.shape[0]
    total = voltages.shape[2] // chans - ntaps + 1
    samples = voltages.astype(jnp.float32).reshape(count, 2, total + ntaps - 1, chans)
    filtered = taps[0][None, None, None, :] * samples[:, :, 0:total, :]
    for tap in range(1, ntaps):
        filtered = filtered + taps[tap][None, None, None, :] * samples[:, :, tap : tap + total, :]
    branch = jnp.arange(chans, dtype=jnp.int32)
    angle = 2.0 * math.pi / chans * (branch[:, None] * branch[None, :] % chans).astype(jnp.float32)
    cosine = jnp.cos(angle)
    sine = jnp.sin(angle)
    high = lax.Precision.HIGHEST
    real_in = filtered[:, 0]
    imag_in = filtered[:, 1]
    real_out = jnp.einsum("asp,pc->acs", real_in, cosine, precision=high) + jnp.einsum(
        "asp,pc->acs", imag_in, sine, precision=high
    )
    imag_out = jnp.einsum("asp,pc->acs", imag_in, cosine, precision=high) - jnp.einsum(
        "asp,pc->acs", real_in, sine, precision=high
    )
    keep = flags.astype(jnp.float32)[:, None, None] / math.sqrt(chans)
    return jnp.stack([real_out * keep, imag_out * keep]).astype(jnp.bfloat16)


def steering(channel, positions, beam_index, chans):
    column = (beam_index % grid_side).astype(jnp.float32)
    row_cell = (beam_index // grid_side).astype(jnp.float32)
    east = (column + 0.5) / grid_side - 0.5
    north = (row_cell + 0.5) / grid_side - 0.5
    ratio = 1.0 + 0.5 * channel.astype(jnp.float32) / chans
    phase = (
        2.0
        * math.pi
        * ratio
        * (positions[0][:, None] * east[None, :] + positions[1][:, None] * north[None, :])
    )
    return (jnp.cos(phase), -jnp.sin(phase))


def form_beams(blocks, channel, positions, beam_index, total, chans):
    high = lax.Precision.HIGHEST
    cov_real = 0.0
    cov_imag = 0.0
    for block in blocks:
        left = jnp.concatenate([block[0], block[1]], axis=1)
        turned = jnp.concatenate([block[1], -block[0]], axis=1)
        cov_real = cov_real + jnp.dot(left, left.T, preferred_element_type=jnp.float32)
        cov_imag = cov_imag + jnp.dot(turned, left.T, preferred_element_type=jnp.float32)
    cov_real = cov_real / total
    cov_imag = cov_imag / total
    count = cov_real.shape[0]
    diagonal = jnp.diagonal(cov_real)
    loading = jnp.mean(diagonal) + 1e-05
    scaling = (damping / (diagonal + loading))[:, None]
    steer_real, steer_imag = steering(channel, positions, beam_index, chans)
    weight_real = scaling * steer_real
    weight_imag = scaling * steer_imag
    for sweep in range(ITERS):
        image_real = (
            jnp.dot(cov_real, weight_real, precision=high)
            - jnp.dot(cov_imag, weight_imag, precision=high)
            + loading * weight_real
        )
        image_imag = (
            jnp.dot(cov_real, weight_imag, precision=high)
            + jnp.dot(cov_imag, weight_real, precision=high)
            + loading * weight_imag
        )
        weight_real = weight_real + scaling * (steer_real - image_real)
        weight_imag = weight_imag + scaling * (steer_imag - image_imag)
    low_real = weight_real.astype(jnp.bfloat16)
    low_imag = weight_imag.astype(jnp.bfloat16)
    plain = jnp.concatenate([low_real, low_imag], axis=0)
    mixed = jnp.concatenate([low_real, -low_imag], axis=0)
    contract = (((0,), (0,)), ((), ()))
    reals = []
    imags = []
    for block in blocks:
        reals.append(
            lax.dot_general(
                plain,
                jnp.concatenate([block[0], block[1]], axis=0),
                contract,
                preferred_element_type=jnp.float32,
            )
        )
        imags.append(
            lax.dot_general(
                mixed,
                jnp.concatenate([block[1], block[0]], axis=0),
                contract,
                preferred_element_type=jnp.float32,
            )
        )
    norm_factor = 1.0 / math.sqrt(count)
    beams = (
        jnp.stack([jnp.concatenate(reals, axis=-1), jnp.concatenate(imags, axis=-1)]) * norm_factor
    )
    return beams.astype(jnp.bfloat16)


def detect(beams):
    floats = beams.astype(jnp.float32)
    energy = floats[:, 0] * floats[:, 0] + floats[:, 1] * floats[:, 1]
    shape = energy.shape
    return energy.reshape(shape[0], shape[1], shape[2] // 4, 4).sum(axis=-1)


def plain(voltages, taps, flags, positions, beam_index):
    spectra = channelize(voltages, taps, flags)
    chans = taps.shape[1]
    per_dev = chans // lax.axis_size("wide")
    first = lax.axis_index("wide") * per_dev
    total = spectra.shape[3]
    pieces = [lax.all_to_all(spectra, "wide", split_axis=2, concat_axis=1, tiled=True)]
    stacked = [jnp.moveaxis(piece, 2, 0) for piece in pieces]

    def one_channel(operands):
        offset, blocks = operands
        return form_beams(blocks, first + offset, positions, beam_index, total, chans)

    beams = lax.map(one_channel, (jnp.arange(per_dev, dtype=jnp.int32), stacked))
    result = lax.all_to_all(
        detect(beams).astype(jnp.bfloat16), "wide", split_axis=1, concat_axis=0, tiled=True
    ).astype(jnp.float32)
    return jnp.transpose(result, (1, 0, 2))


MESH = pl.DeviceIdType.MESH
LANES = 128
ROWS = 16
NT = (((1,), (1,)), ((), ()))


def cosine_turns(turns):
    frac = jnp.abs(turns - jnp.floor(turns + 0.5))
    x = (0.25 - frac) * (2.0 * math.pi)
    sq = x * x
    poly = -1.0 / 39916800.0
    for term in (1.0 / 362880.0, -1.0 / 5040.0, 1.0 / 120.0, -1.0 / 6.0, 1.0):
        poly = poly * sq + term
    return x * poly


def swap_halves(block):
    return pltpu.roll(block, LANES // 2, 1)


def kernel(
    volt_hbm, taps_hbm, flags_hbm, place_hbm, index_hbm, out_ref,
    volt, taps_ref, flags_ref, place_ref, index_ref, bank, mixed, sent, spec, steer, weight, low, image, applied, scale,
    tell, told, give, got,
    volt_sem, send_sem, recv_sem, tell_sem, told_sem, give_sem, got_sem,
    *, wide, total, chans, window, bounds, early,
):
    me = lax.axis_index("wide")
    parts = len(bounds) - 1
    beams = index_hbm.shape[1]
    width = wide * LANES
    hop = ROWS * chans
    length = volt_hbm.shape[2]
    ntaps = taps_hbm.shape[0]
    half_lanes = LANES // 2

    barrier = pltpu.get_barrier_semaphore()
    first_reach = bounds[1] * chans + window - hop
    loads = [
        pltpu.make_async_copy(source, target, volt_sem.at[at])
        for at, (source, target) in enumerate(
            [
                (taps_hbm, taps_ref),
                (flags_hbm, flags_ref),
                (place_hbm, place_ref),
                (index_hbm, index_ref),
                (volt_hbm.at[:, :, :first_reach], volt.at[:, :, :first_reach]),
                (volt_hbm.at[:, :, first_reach:], volt.at[:, :, first_reach:]),
            ]
        )
    ]
    for load in loads:
        load.start()

    def greet(off, carry):
        pl.semaphore_signal(
            barrier, inc=1, device_id={"wide": lax.rem(me + off, wide)}, device_id_type=MESH
        )
        return carry

    lax.fori_loop(1, wide, greet, 0)

    ranked = sorted(range(1, wide), key=lambda off: (abs(off - wide // 2), off))
    cut = (len(ranked) + 1) // 2
    mixed_order = [
        entry for duo in zip(ranked[:cut], ranked[cut:] + [None]) for entry in duo
    ]
    mixed_order = [entry for entry in mixed_order if entry is not None]
    turned_order = list(mixed_order)
    for at in range(0, len(turned_order) - 1, 2):
        turned_order[at], turned_order[at + 1] = turned_order[at + 1], turned_order[at]

    def everyone(act):
        core = lax.rem(me, 2)
        for one, two in zip(mixed_order, turned_order):
            act(lax.rem(me + (one + core * (two - one)), wide))

    def iota(shape, axis):
        return lax.broadcasted_iota(jnp.int32, shape, axis)

    for load in loads[:4]:
        load.wait()
    slot = iota((ROWS, window), 1) // chans
    delay = slot - iota((ROWS, window), 0)
    spread = jnp.where(iota((chans, window), 1) % chans == iota((chans, window), 0), 1.0, 0.0)
    tiled = jnp.dot(
        taps_ref[...], spread, precision=lax.Precision.HIGHEST, preferred_element_type=jnp.float32
    )
    filt = jnp.zeros((ROWS, window), jnp.float32)
    for tap in range(ntaps):
        filt = filt + jnp.where(delay == tap, tiled[tap : tap + 1, :], 0.0)
    spin = (iota((chans, window), 0) * (iota((chans, window), 1) % chans)) % chans
    spin = spin.astype(jnp.float32) / chans
    for half in range(2):
        wave = cosine_turns(spin - 0.25 * half) / math.sqrt(chans)
        for channel in range(chans):
            entry = wave[channel : channel + 1, :] * filt
            top = entry.astype(jnp.bfloat16)
            rest = (entry - top.astype(jnp.float32)).astype(jnp.bfloat16)
            cols = slice(half * window, (half + 1) * window)
            bank[channel * ROWS : (channel + 1) * ROWS, cols] = top
            bank[hop + channel * ROWS : hop + (channel + 1) * ROWS, cols] = rest

    doubled = jnp.where(iota((half_lanes, LANES), 1) // 2 == iota((half_lanes, LANES), 0), 1.0, 0.0)
    keep = jnp.broadcast_to(flags_ref[...].astype(jnp.float32), (8, half_lanes))
    keep = jnp.dot(
        keep.astype(jnp.bfloat16), doubled.astype(jnp.bfloat16), preferred_element_type=jnp.float32
    )[0:1]
    row = iota((2 * LANES, LANES), 0)
    antenna = row % half_lanes
    quarter = row // half_lanes
    from_part = jnp.where((quarter == 1) | (quarter == 2), 1, 0)
    chosen = iota((2 * LANES, LANES), 1) == 2 * antenna + from_part
    order = jnp.where(chosen, jnp.where(quarter == 3, -keep, keep), 0.0).astype(jnp.bfloat16)

    def mix(start, size):
        block = volt[:, :, start : start + size].reshape(LANES, size)
        mixed[:, start : start + size] = jnp.dot(
            order, block, preferred_element_type=jnp.float32
        ).astype(jnp.bfloat16)

    def rows_of(part):
        return slice(bounds[part], bounds[part + 1])

    def lanes_of(block):
        return pl.ds(pl.multiple_of(block * LANES, LANES), LANES)

    def remote(source, target, out_sem, in_sem, other):
        return pltpu.make_async_remote_copy(
            src_ref=source,
            dst_ref=target,
            send_sem=out_sem,
            recv_sem=in_sem,
            device_id={"wide": other},
            device_id_type=MESH,
        )

    def await_bytes(ref, sem):
        pltpu.make_async_copy(ref, ref, sem).wait()

    def ship(part):
        rows = rows_of(part)
        everyone(
            lambda other: remote(
                sent.at[other, rows, :], spec.at[me, rows, :],
                send_sem.at[part], recv_sem.at[part], other,
            ).start()
        )
        pltpu.make_async_copy(
            sent.at[me, rows, :], spec.at[me, rows, :], recv_sem.at[part]
        ).start()

    tell[...] = jnp.zeros_like(tell)

    def channelize_pair(pair, carry):
        start = pl.multiple_of(pair * (2 * hop), LANES)
        both = jnp.concatenate(
            [
                jnp.concatenate(
                    [mixed[:LANES, pl.ds(at, window)], mixed[LANES:, pl.ds(at, window)]], axis=1
                )
                for at in (start, pl.multiple_of(start + hop, LANES))
            ],
            axis=0,
        )
        acc = lax.dot_general(bank[...], both, NT, preferred_element_type=jnp.float32)
        rounded = (acc[:hop] + acc[hop:]).astype(jnp.bfloat16)
        for side in range(2):
            at = pl.multiple_of(pair * (2 * ROWS) + side * ROWS, ROWS)
            block = rounded[:, side * LANES : (side + 1) * LANES].reshape(chans, ROWS, LANES)
            sent[:, pl.ds(at, ROWS), :] = block
            block = block.astype(jnp.float32)
            block = block * block
            tell[...] += block[:, :8] + block[:, 8:]
        return carry

    loads[4].wait()
    tail = length // LANES * LANES
    mixed[:, tail:] = jnp.zeros((2 * LANES, mixed.shape[1] - tail), jnp.bfloat16)
    over = window - hop
    reach = 0
    for part in range(parts):
        if part == 1:
            loads[5].wait()
        upto = min(bounds[part + 1] * chans + over, length)
        mix(reach, upto - reach)
        reach = upto
        span = 2 * ROWS
        lax.fori_loop(bounds[part] // span, bounds[part + 1] // span, channelize_pair, 0)
        if part == 0:
            pl.semaphore_wait(barrier, wide - 1)
        if part < early:
            ship(part)
    everyone(
        lambda other: remote(
            tell.at[other], told.at[me], tell_sem.at[0], told_sem.at[0], other
        ).start()
    )
    pltpu.make_async_copy(tell.at[me], told.at[me], told_sem.at[0]).start()
    for part in range(early, parts):
        ship(part)

    index = index_ref[...]
    ratio = 1.0 + 0.5 * me.astype(jnp.float32) / chans
    cells = [
        ((index % grid_side).astype(jnp.float32) + 0.5) / grid_side - 0.5,
        ((index // grid_side).astype(jnp.float32) + 0.5) / grid_side - 0.5,
    ]
    same = iota((beams, beams), 0) == iota((beams, beams), 1)
    east, north = [
        jnp.sum(jnp.where(same, cell, 0.0), axis=1, keepdims=True) * ratio for cell in cells
    ]
    first_half = iota((1, LANES), 1) < half_lanes
    turn = jnp.where(first_half, 0.0, 0.25)

    def steer_duo(duo, carry):
        here = place_ref[:, lanes_of(duo)]
        here = jnp.concatenate([here, jnp.zeros((6, LANES), jnp.float32)], axis=0)
        there = swap_halves(here)
        for side in range(2):
            both = jnp.where(first_half, here, there) if side == 0 else jnp.where(
                first_half, there, here
            )
            turns = east * both[0:1] + north * both[1:2] + turn
            steer[:, lanes_of(2 * duo + side)] = cosine_turns(turns)
        return carry

    lax.fori_loop(0, wide // 2, steer_duo, 0)

    await_bytes(told, told_sem.at[0])
    sign = jnp.where(first_half, 1.0, -1.0)
    power = jnp.sum(told[...], axis=1, keepdims=True) * (1.0 / total)
    loading = jnp.sum(power) / (width // 2) + 1e-05
    for block in range(wide):
        piece = jnp.broadcast_to(power[block], (8, LANES))
        piece = piece + swap_halves(piece)
        scale[:, block * LANES : (block + 1) * LANES] = 0.5 / (piece + loading)

    def keep_low(lanes, value):
        low[:beams, lanes] = value.astype(jnp.bfloat16)
        low[beams:, lanes] = (swap_halves(value) * sign).astype(jnp.bfloat16)

    def first_block(block, carry):
        lanes = lanes_of(block)
        value = scale[0:1, lanes] * steer[:, lanes]
        weight[:, lanes] = value
        keep_low(lanes, value)
        return carry

    lax.fori_loop(0, wide, first_block, 0)

    def project(rows):
        strip = jnp.concatenate([spec[block, rows, :] for block in range(wide)], axis=1)
        return lax.dot_general(low[...], strip, NT, preferred_element_type=jnp.float32)

    def back_project(rows, last, sweep, first):
        def duo_block(duo, carry):
            strip = jnp.concatenate([spec[2 * duo, rows, :], spec[2 * duo + 1, rows, :]], axis=1)
            back = jnp.dot(image[:, rows], strip, preferred_element_type=jnp.float32)
            for side in range(2):
                lanes = lanes_of(2 * duo + side)
                cols = slice(side * LANES, (side + 1) * LANES)
                fresh = back[:beams, cols] - sign * swap_halves(back[beams:, cols])
                if not first:
                    fresh = applied[:, lanes] + fresh
                if not last:
                    applied[:, lanes] = fresh
                    continue
                value = weight[:, lanes]
                value = value + scale[0:1, lanes] * (
                    steer[:, lanes] - (fresh * (1.0 / total) + loading * value)
                )
                if sweep < ITERS - 1:
                    weight[:, lanes] = value
                keep_low(lanes, value)
            return carry

        lax.fori_loop(0, wide // 2, duo_block, 0)

    for part in range(parts):
        rows = rows_of(part)
        await_bytes(spec.at[:, rows, :], recv_sem.at[part])
        if bounds[part + 1] % (total // 2):
            continue
        rows = slice(bounds[part + 1] - total // 2, bounds[part + 1])
        image[:, rows] = project(rows).astype(jnp.bfloat16)
        back_project(rows, part + 1 == parts, 0, rows.start == 0)

    half_rows = total // 2
    halves = [slice(half * half_rows, (half + 1) * half_rows) for half in range(2)]
    for sweep in range(1, ITERS):
        for rows in halves:
            image[:, rows] = project(rows).astype(jnp.bfloat16)
        back_project(slice(0, total), True, sweep, True)

    group = total // 4
    share = give.shape[1]
    sums = jnp.zeros((beams, group), jnp.float32)
    for half, rows in enumerate(halves):
        value = project(rows)
        energy = value[:beams] * value[:beams] + value[beams:] * value[beams:]
        energy = energy * (2.0 / width)
        top = energy.astype(jnp.bfloat16)
        rest = (energy - top.astype(jnp.float32)).astype(jnp.bfloat16)
        source = iota((half_rows, group), 0) + half * half_rows
        target = iota((half_rows, group), 1) * 4
        pick = jnp.where((source >= target) & (source < target + 4), 1.0, 0.0)
        pick = pick.astype(jnp.bfloat16)
        sums = sums + jnp.dot(top, pick, preferred_element_type=jnp.float32)
        sums = sums + jnp.dot(rest, pick, preferred_element_type=jnp.float32)
    give[...] = sums.astype(jnp.bfloat16).reshape(wide, share, group)
    everyone(
        lambda other: remote(
            give.at[other], got.at[me], give_sem.at[0], got_sem.at[0], other
        ).start()
    )
    pltpu.make_async_copy(give.at[me], got.at[me], got_sem.at[0]).start()
    for part in range(parts):
        await_bytes(sent.at[: wide - 1, rows_of(part), :], send_sem.at[part])
    await_bytes(tell.at[: wide - 1], tell_sem.at[0])
    await_bytes(got, got_sem.at[0])
    for channel in range(chans):
        out_ref[:, channel, :] = got[channel].astype(jnp.float32)
    await_bytes(give.at[: wide - 1], give_sem.at[0])


def fused(voltages, taps, flags, positions, beam_index):
    wide = lax.axis_size("wide")
    count, _, length = voltages.shape
    ntaps, chans = taps.shape
    total = length // chans - ntaps + 1
    beams = beam_index.shape[0]
    hop = ROWS * chans
    window = -(-(ROWS + ntaps - 1) * chans // LANES) * LANES
    padded = (total // ROWS - 1) * hop + window
    bounds = [0, LANES // 2] + list(range(LANES, total + 1, LANES))
    parts = len(bounds) - 1
    share = beams // wide
    width = wide * LANES
    vmem = pl.BlockSpec(memory_space=pltpu.VMEM)
    return pl.pallas_call(
        functools.partial(
            kernel, wide=wide, total=total, chans=chans, window=window, bounds=bounds,
            early=min(3, parts),
        ),
        out_shape=jax.ShapeDtypeStruct((share, chans, total // 4), jnp.float32),
        in_specs=[pl.BlockSpec(memory_space=pl.ANY)] * 5,
        out_specs=vmem,
        scratch_shapes=[
            pltpu.VMEM(voltages.shape, jnp.bfloat16),
            pltpu.VMEM(taps.shape, jnp.float32),
            pltpu.VMEM((1, count), jnp.int32),
            pltpu.VMEM(positions.shape, jnp.float32),
            pltpu.VMEM((1, beams), jnp.int32),
            pltpu.VMEM((2 * hop, 2 * window), jnp.bfloat16),
            pltpu.VMEM((2 * LANES, padded), jnp.bfloat16),
            pltpu.VMEM((chans, total, LANES), jnp.bfloat16),
            pltpu.VMEM((wide, total, LANES), jnp.bfloat16),
            pltpu.VMEM((beams, width), jnp.float32),
            pltpu.VMEM((beams, width), jnp.float32),
            pltpu.VMEM((2 * beams, width), jnp.bfloat16),
            pltpu.VMEM((2 * beams, total), jnp.bfloat16),
            pltpu.VMEM((beams, width), jnp.float32),
            pltpu.VMEM((8, width), jnp.float32),
            pltpu.VMEM((chans, 8, LANES), jnp.float32),
            pltpu.VMEM((wide, 8, LANES), jnp.float32),
            pltpu.VMEM((wide, share, total // 4), jnp.bfloat16),
            pltpu.VMEM((chans, share, total // 4), jnp.bfloat16),
            pltpu.SemaphoreType.DMA((6,)),
            pltpu.SemaphoreType.DMA((parts,)),
            pltpu.SemaphoreType.DMA((parts,)),
            pltpu.SemaphoreType.DMA((1,)),
            pltpu.SemaphoreType.DMA((1,)),
            pltpu.SemaphoreType.DMA((1,)),
            pltpu.SemaphoreType.DMA((1,)),
        ],
        compiler_params=pltpu.CompilerParams(
            collective_id=0, has_side_effects=True, vmem_limit_bytes=64 * 2**20 - 2**16
        ),
    )(voltages, taps, flags.reshape(1, -1), positions, beam_index.reshape(1, -1))


def fits(voltages, taps, beam_index, wide):
    count, _, length = voltages.shape
    ntaps, chans = taps.shape
    total = length // chans - ntaps + 1
    return (
        2 * count == LANES
        and chans == wide
        and (ROWS * chans) % LANES == 0
        and wide % 2 == 0
        and total % 256 == 0
        and beam_index.shape[0] % (ROWS * wide) == 0
        and (total // 4) % LANES == 0
    )


def local(voltages, taps, flags, positions, beam_index):
    if fits(voltages, taps, beam_index, lax.axis_size("wide")):
        return fused(voltages, taps, flags, positions, beam_index)
    return plain(voltages, taps, flags, positions, beam_index)


def solution(mesh):
    in_specs = (P(("grp", "wide"), None, None), P(), P(("grp", "wide")), P(), P("grp"))
    out_specs = P(("grp", "wide"), None, None)
    return jax.shard_map(local, mesh=mesh, in_specs=in_specs, out_specs=out_specs, check_vma=False)
```

```python
import functools
import math

import jax
import jax.numpy as jnp
import numpy as np
from jax import lax
from jax.experimental import pallas as pl
from jax.experimental.pallas import tpu as pltpu
from jax.sharding import PartitionSpec as P

ITERS = 2


damping = 0.5
grid_side = 32


def channelize(voltages, taps, flags):
    count = voltages.shape[0]
    chans = taps.shape[1]
    ntaps = taps.shape[0]
    total = voltages.shape[2] // chans - ntaps + 1
    samples = voltages.astype(jnp.float32).reshape(count, 2, total + ntaps - 1, chans)
    filtered = taps[0][None, None, None, :] * samples[:, :, 0:total, :]
    for tap in range(1, ntaps):
        filtered = filtered + taps[tap][None, None, None, :] * samples[:, :, tap : tap + total, :]
    branch = jnp.arange(chans, dtype=jnp.int32)
    angle = 2.0 * math.pi / chans * (branch[:, None] * branch[None, :] % chans).astype(jnp.float32)
    cosine = jnp.cos(angle)
    sine = jnp.sin(angle)
    high = lax.Precision.HIGHEST
    real_in = filtered[:, 0]
    imag_in = filtered[:, 1]
    real_out = jnp.einsum("asp,pc->acs", real_in, cosine, precision=high) + jnp.einsum(
        "asp,pc->acs", imag_in, sine, precision=high
    )
    imag_out = jnp.einsum("asp,pc->acs", imag_in, cosine, precision=high) - jnp.einsum(
        "asp,pc->acs", real_in, sine, precision=high
    )
    keep = flags.astype(jnp.float32)[:, None, None] / math.sqrt(chans)
    return jnp.stack([real_out * keep, imag_out * keep]).astype(jnp.bfloat16)


def steering(channel, positions, beam_index, chans):
    column = (beam_index % grid_side).astype(jnp.float32)
    row_cell = (beam_index // grid_side).astype(jnp.float32)
    east = (column + 0.5) / grid_side - 0.5
    north = (row_cell + 0.5) / grid_side - 0.5
    ratio = 1.0 + 0.5 * channel.astype(jnp.float32) / chans
    phase = (
        2.0
        * math.pi
        * ratio
        * (positions[0][:, None] * east[None, :] + positions[1][:, None] * north[None, :])
    )
    return (jnp.cos(phase), -jnp.sin(phase))


def form_beams(blocks, channel, positions, beam_index, total, chans):
    high = lax.Precision.HIGHEST
    cov_real = 0.0
    cov_imag = 0.0
    for block in blocks:
        left = jnp.concatenate([block[0], block[1]], axis=1)
        turned = jnp.concatenate([block[1], -block[0]], axis=1)
        cov_real = cov_real + jnp.dot(left, left.T, preferred_element_type=jnp.float32)
        cov_imag = cov_imag + jnp.dot(turned, left.T, preferred_element_type=jnp.float32)
    cov_real = cov_real / total
    cov_imag = cov_imag / total
    count = cov_real.shape[0]
    diagonal = jnp.diagonal(cov_real)
    loading = jnp.mean(diagonal) + 1e-05
    scaling = (damping / (diagonal + loading))[:, None]
    steer_real, steer_imag = steering(channel, positions, beam_index, chans)
    weight_real = scaling * steer_real
    weight_imag = scaling * steer_imag
    for sweep in range(ITERS):
        image_real = (
            jnp.dot(cov_real, weight_real, precision=high)
            - jnp.dot(cov_imag, weight_imag, precision=high)
            + loading * weight_real
        )
        image_imag = (
            jnp.dot(cov_real, weight_imag, precision=high)
            + jnp.dot(cov_imag, weight_real, precision=high)
            + loading * weight_imag
        )
        weight_real = weight_real + scaling * (steer_real - image_real)
        weight_imag = weight_imag + scaling * (steer_imag - image_imag)
    low_real = weight_real.astype(jnp.bfloat16)
    low_imag = weight_imag.astype(jnp.bfloat16)
    plain = jnp.concatenate([low_real, low_imag], axis=0)
    mixed = jnp.concatenate([low_real, -low_imag], axis=0)
    contract = (((0,), (0,)), ((), ()))
    reals = []
    imags = []
    for block in blocks:
        reals.append(
            lax.dot_general(
                plain,
                jnp.concatenate([block[0], block[1]], axis=0),
                contract,
                preferred_element_type=jnp.float32,
            )
        )
        imags.append(
            lax.dot_general(
                mixed,
                jnp.concatenate([block[1], block[0]], axis=0),
                contract,
                preferred_element_type=jnp.float32,
            )
        )
    norm_factor = 1.0 / math.sqrt(count)
    beams = (
        jnp.stack([jnp.concatenate(reals, axis=-1), jnp.concatenate(imags, axis=-1)]) * norm_factor
    )
    return beams.astype(jnp.bfloat16)


def detect(beams):
    floats = beams.astype(jnp.float32)
    energy = floats[:, 0] * floats[:, 0] + floats[:, 1] * floats[:, 1]
    shape = energy.shape
    return energy.reshape(shape[0], shape[1], shape[2] // 4, 4).sum(axis=-1)


def plain(voltages, taps, flags, positions, beam_index):
    spectra = channelize(voltages, taps, flags)
    chans = taps.shape[1]
    per_dev = chans // lax.axis_size("wide")
    first = lax.axis_index("wide") * per_dev
    total = spectra.shape[3]
    pieces = [lax.all_to_all(spectra, "wide", split_axis=2, concat_axis=1, tiled=True)]
    stacked = [jnp.moveaxis(piece, 2, 0) for piece in pieces]

    def one_channel(operands):
        offset, blocks = operands
        return form_beams(blocks, first + offset, positions, beam_index, total, chans)

    beams = lax.map(one_channel, (jnp.arange(per_dev, dtype=jnp.int32), stacked))
    result = lax.all_to_all(
        detect(beams).astype(jnp.bfloat16), "wide", split_axis=1, concat_axis=0, tiled=True
    ).astype(jnp.float32)
    return jnp.transpose(result, (1, 0, 2))


MESH = pl.DeviceIdType.MESH
LANES = 128
ROWS = 16
CHUNK = 256
NT = (((1,), (1,)), ((), ()))


def cosine_turns(turns):
    frac = jnp.abs(turns - jnp.floor(turns + 0.5))
    x = (0.25 - frac) * (2.0 * math.pi)
    sq = x * x
    poly = -1.0 / 39916800.0
    for term in (1.0 / 362880.0, -1.0 / 5040.0, 1.0 / 120.0, -1.0 / 6.0, 1.0):
        poly = poly * sq + term
    return x * poly


def swap_halves(block):
    return pltpu.roll(block, LANES // 2, 1)


def kernel(
    volt_hbm, taps_hbm, flags_hbm, place_hbm, index_hbm, out_ref,
    volt, taps_ref, flags_ref, place_ref, index_ref, bank, order, mixed, sent, spec, steer, weight, low, whole, image, applied, scale, sums,
    tell, told, give, got,
    volt_sem, send_sem, recv_sem, tell_sem, told_sem, give_sem, got_sem,
    *, wide, total, chans, window, parts, early,
):
    me = lax.axis_index("wide")
    step = total // parts
    beams = index_hbm.shape[1]
    width = wide * LANES
    hop = ROWS * chans
    length = volt_hbm.shape[2]
    ntaps = taps_hbm.shape[0]
    half_lanes = LANES // 2

    barrier = pltpu.get_barrier_semaphore()
    first_reach = min(step * chans + CHUNK, length // CHUNK * CHUNK)
    loads = [
        pltpu.make_async_copy(source, target, volt_sem.at[at])
        for at, (source, target) in enumerate(
            [
                (taps_hbm, taps_ref),
                (flags_hbm, flags_ref),
                (place_hbm, place_ref),
                (index_hbm, index_ref),
                (volt_hbm.at[:, :, :first_reach], volt.at[:, :, :first_reach]),
                (volt_hbm.at[:, :, first_reach:], volt.at[:, :, first_reach:]),
            ]
        )
    ]
    for load in loads:
        load.start()

    def greet(off, carry):
        pl.semaphore_signal(
            barrier, inc=1, device_id={"wide": lax.rem(me + off, wide)}, device_id_type=MESH
        )
        return carry

    lax.fori_loop(1, wide, greet, 0)

    def everyone(act):
        def body(turn, carry):
            off = 1 + lax.rem((turn + lax.rem(me, 2)) * (wide // 2 - 1), wide - 1)
            act(lax.rem(me + off, wide))
            return carry

        lax.fori_loop(0, wide - 1, body, 0)

    def iota(shape, axis):
        return lax.broadcasted_iota(jnp.int32, shape, axis)

    for load in loads[:4]:
        load.wait()
    slot = iota((ROWS, window), 1) // chans
    delay = slot - iota((ROWS, window), 0)
    spread = jnp.where(iota((chans, window), 1) % chans == iota((chans, window), 0), 1.0, 0.0)
    tiled = jnp.dot(
        taps_ref[...], spread, precision=lax.Precision.HIGHEST, preferred_element_type=jnp.float32
    )
    filt = jnp.zeros((ROWS, window), jnp.float32)
    for tap in range(ntaps):
        filt = filt + jnp.where(delay == tap, tiled[tap : tap + 1, :], 0.0)
    spin = (iota((chans, window), 0) * (iota((chans, window), 1) % chans)) % chans
    spin = spin.astype(jnp.float32) / chans
    for half in range(2):
        wave = cosine_turns(spin - 0.25 * half) / math.sqrt(chans)
        for channel in range(chans):
            entry = wave[channel : channel + 1, :] * filt
            top = entry.astype(jnp.bfloat16)
            rest = (entry - top.astype(jnp.float32)).astype(jnp.bfloat16)
            cols = slice(half * window, (half + 1) * window)
            bank[channel * ROWS : (channel + 1) * ROWS, cols] = top
            bank[hop + channel * ROWS : hop + (channel + 1) * ROWS, cols] = rest

    doubled = jnp.where(iota((half_lanes, LANES), 1) // 2 == iota((half_lanes, LANES), 0), 1.0, 0.0)
    keep = jnp.broadcast_to(flags_ref[...].astype(jnp.float32), (8, half_lanes))
    keep = jnp.dot(
        keep.astype(jnp.bfloat16), doubled.astype(jnp.bfloat16), preferred_element_type=jnp.float32
    )[0:1]
    row = iota((2 * LANES, LANES), 0)
    antenna = row % half_lanes
    quarter = row // half_lanes
    from_part = jnp.where((quarter == 1) | (quarter == 2), 1, 0)
    chosen = iota((2 * LANES, LANES), 1) == 2 * antenna + from_part
    order[...] = jnp.where(chosen, jnp.where(quarter == 3, -keep, keep), 0.0).astype(jnp.bfloat16)

    def mix(start, size):
        lanes = pl.ds(start, size)
        block = volt[:, :, lanes].reshape(LANES, size)
        mixed[:, lanes] = jnp.dot(
            order[...], block, preferred_element_type=jnp.float32
        ).astype(jnp.bfloat16)

    def mix_chunk(chunk, carry):
        mix(pl.multiple_of(chunk * CHUNK, CHUNK), CHUNK)
        return carry

    def rows_of(part):
        return pl.ds(pl.multiple_of(part * step, step), step)

    def lanes_of(block):
        return pl.ds(pl.multiple_of(block * LANES, LANES), LANES)

    def remote(source, target, out_sem, in_sem, other):
        return pltpu.make_async_remote_copy(
            src_ref=source,
            dst_ref=target,
            send_sem=out_sem,
            recv_sem=in_sem,
            device_id={"wide": other},
            device_id_type=MESH,
        )

    def await_bytes(ref, sem):
        pltpu.make_async_copy(ref, ref, sem).wait()

    def ship(part):
        rows = rows_of(part)
        everyone(
            lambda other: remote(
                sent.at[other, rows, :], spec.at[me, rows, :],
                send_sem.at[part], recv_sem.at[part], other,
            ).start()
        )
        pltpu.make_async_copy(
            sent.at[me, rows, :], spec.at[me, rows, :], recv_sem.at[part]
        ).start()

    tell[...] = jnp.zeros_like(tell)

    def channelize_pair(pair, carry):
        start = pl.multiple_of(pair * (2 * hop), LANES)
        both = jnp.concatenate(
            [
                jnp.concatenate(
                    [mixed[:LANES, pl.ds(at, window)], mixed[LANES:, pl.ds(at, window)]], axis=1
                )
                for at in (start, pl.multiple_of(start + hop, LANES))
            ],
            axis=0,
        )
        acc = lax.dot_general(bank[...], both, NT, preferred_element_type=jnp.float32)
        rounded = (acc[:hop] + acc[hop:]).astype(jnp.bfloat16)
        for side in range(2):
            at = pl.multiple_of(pair * (2 * ROWS) + side * ROWS, ROWS)
            block = rounded[:, side * LANES : (side + 1) * LANES].reshape(chans, ROWS, LANES)
            sent[:, pl.ds(at, ROWS), :] = block
            block = block.astype(jnp.float32)
            block = block * block
            tell[...] += block[:, :8] + block[:, 8:]
        return carry

    chunks = length // CHUNK
    tail = chunks * CHUNK
    loads[4].wait()
    mixed[:, tail:] = jnp.zeros((2 * LANES, mixed.shape[1] - tail), jnp.bfloat16)
    lead = first_reach // CHUNK
    ahead = step * chans // CHUNK
    lax.fori_loop(0, lead - ahead, mix_chunk, 0)

    def produce(part, carry):
        @pl.when(part == 1)
        def _():
            loads[5].wait()
            mix(tail, length - tail)

        begin = jnp.minimum(lead - ahead + part * ahead, chunks)
        lax.fori_loop(begin, jnp.minimum(begin + ahead, chunks), mix_chunk, 0)
        pairs = step // (2 * ROWS)
        lax.fori_loop(part * pairs, (part + 1) * pairs, channelize_pair, 0)

        @pl.when(part == 0)
        def _():
            pl.semaphore_wait(barrier, wide - 1)

        @pl.when(part < early)
        def _():
            ship(part)

        return carry

    lax.fori_loop(0, parts, produce, 0)
    everyone(
        lambda other: remote(
            tell.at[other], told.at[me], tell_sem.at[0], told_sem.at[0], other
        ).start()
    )
    pltpu.make_async_copy(tell.at[me], told.at[me], told_sem.at[0]).start()

    def ship_late(part, carry):
        ship(part)
        return carry

    lax.fori_loop(early, parts, ship_late, 0)

    index = index_ref[...]
    ratio = 1.0 + 0.5 * me.astype(jnp.float32) / chans
    cells = [
        ((index % grid_side).astype(jnp.float32) + 0.5) / grid_side - 0.5,
        ((index // grid_side).astype(jnp.float32) + 0.5) / grid_side - 0.5,
    ]
    same = iota((beams, beams), 0) == iota((beams, beams), 1)
    east, north = [
        jnp.sum(jnp.where(same, cell, 0.0), axis=1, keepdims=True) * ratio for cell in cells
    ]
    first_half = iota((1, LANES), 1) < half_lanes
    turn = jnp.where(first_half, 0.0, 0.25)

    def steer_duo(duo, carry):
        here = place_ref[:, lanes_of(duo)]
        here = jnp.concatenate([here, jnp.zeros((6, LANES), jnp.float32)], axis=0)
        there = swap_halves(here)
        for side in range(2):
            both = jnp.where(first_half, here, there) if side == 0 else jnp.where(
                first_half, there, here
            )
            turns = east * both[0:1] + north * both[1:2] + turn
            steer[:, lanes_of(2 * duo + side)] = cosine_turns(turns)
        return carry

    lax.fori_loop(0, wide // 2, steer_duo, 0)

    await_bytes(told, told_sem.at[0])
    sign = jnp.where(first_half, 1.0, -1.0)
    power = jnp.sum(told[...], axis=1, keepdims=True) * (1.0 / total)
    loading = jnp.sum(power) / (width // 2) + 1e-05
    for block in range(wide):
        piece = jnp.broadcast_to(power[block], (8, LANES))
        piece = piece + swap_halves(piece)
        scale[:, block * LANES : (block + 1) * LANES] = 0.5 / (piece + loading)

    def keep_low(lanes, value):
        low[:beams, lanes] = value.astype(jnp.bfloat16)
        low[beams:, lanes] = (swap_halves(value) * sign).astype(jnp.bfloat16)

    def first_block(block, carry):
        lanes = lanes_of(block)
        value = scale[0:1, lanes] * steer[:, lanes]
        weight[:, lanes] = value
        keep_low(lanes, value)
        return carry

    lax.fori_loop(0, wide, first_block, 0)

    half_rows = total // 2
    group = total // 4
    share = give.shape[1]

    def stage_half(turn, carry):
        stage = turn // 2
        half = turn % 2
        rows = pl.ds(pl.multiple_of(half * half_rows, half_rows), half_rows)

        @pl.when(stage == 0)
        def _():
            def land(part, carry):
                await_bytes(spec.at[:, rows_of(part), :], recv_sem.at[part])
                return carry

            lax.fori_loop(half * (parts // 2), (half + 1) * (parts // 2), land, 0)

        strip = jnp.concatenate([spec[block, rows, :] for block in range(wide)], axis=1)
        whole[...] = lax.dot_general(low[...], strip, NT, preferred_element_type=jnp.float32)

        @pl.when(stage < ITERS)
        def _():
            image[...] = whole[...].astype(jnp.bfloat16)

            def duo_block(duo, carry):
                strip = jnp.concatenate(
                    [spec[2 * duo, rows, :], spec[2 * duo + 1, rows, :]], axis=1
                )
                back = jnp.dot(image[...], strip, preferred_element_type=jnp.float32)
                for side in range(2):
                    lanes = lanes_of(2 * duo + side)
                    cols = slice(side * LANES, (side + 1) * LANES)
                    fresh = back[:beams, cols] - sign * swap_halves(back[beams:, cols])

                    @pl.when(half == 0)
                    def _():
                        applied[:, lanes] = fresh

                    @pl.when(half == 1)
                    def _():
                        value = weight[:, lanes]
                        value = value + scale[0:1, lanes] * (
                            steer[:, lanes]
                            - ((applied[:, lanes] + fresh) * (1.0 / total) + loading * value)
                        )
                        weight[:, lanes] = value
                        keep_low(lanes, value)

                return carry

            lax.fori_loop(0, wide // 2, duo_block, 0)

        @pl.when(stage == ITERS)
        def _():
            value = whole[...]
            energy = value[:beams] * value[:beams] + value[beams:] * value[beams:]
            energy = energy * (2.0 / width)
            top = energy.astype(jnp.bfloat16)
            rest = (energy - top.astype(jnp.float32)).astype(jnp.bfloat16)
            source = iota((half_rows, group), 0) + half * half_rows
            target = iota((half_rows, group), 1) * 4
            pick = jnp.where((source >= target) & (source < target + 4), 1.0, 0.0)
            pick = pick.astype(jnp.bfloat16)
            sums[...] += jnp.dot(top, pick, preferred_element_type=jnp.float32) + jnp.dot(
                rest, pick, preferred_element_type=jnp.float32
            )

        return carry

    sums[...] = jnp.zeros_like(sums)
    lax.fori_loop(0, 2 * (ITERS + 1), stage_half, 0)
    give[...] = sums[...].astype(jnp.bfloat16).reshape(wide, share, group)
    everyone(
        lambda other: remote(
            give.at[other], got.at[me], give_sem.at[0], got_sem.at[0], other
        ).start()
    )
    pltpu.make_async_copy(give.at[me], got.at[me], got_sem.at[0]).start()

    def settle(part, carry):
        await_bytes(sent.at[: wide - 1, rows_of(part), :], send_sem.at[part])
        return carry

    lax.fori_loop(0, parts, settle, 0)
    await_bytes(tell.at[: wide - 1], tell_sem.at[0])
    await_bytes(got, got_sem.at[0])
    for channel in range(chans):
        out_ref[:, channel, :] = got[channel].astype(jnp.float32)
    await_bytes(give.at[: wide - 1], give_sem.at[0])


def fused(voltages, taps, flags, positions, beam_index):
    wide = lax.axis_size("wide")
    count, _, length = voltages.shape
    ntaps, chans = taps.shape
    total = length // chans - ntaps + 1
    beams = beam_index.shape[0]
    hop = ROWS * chans
    window = -(-(ROWS + ntaps - 1) * chans // LANES) * LANES
    padded = (total // ROWS - 1) * hop + window
    parts = 8
    share = beams // wide
    width = wide * LANES
    vmem = pl.BlockSpec(memory_space=pltpu.VMEM)
    return pl.pallas_call(
        functools.partial(
            kernel, wide=wide, total=total, chans=chans, window=window, parts=parts,
            early=parts // 2,
        ),
        out_shape=jax.ShapeDtypeStruct((share, chans, total // 4), jnp.float32),
        in_specs=[pl.BlockSpec(memory_space=pl.ANY)] * 5,
        out_specs=vmem,
        scratch_shapes=[
            pltpu.VMEM(voltages.shape, jnp.bfloat16),
            pltpu.VMEM(taps.shape, jnp.float32),
            pltpu.VMEM((1, count), jnp.int32),
            pltpu.VMEM(positions.shape, jnp.float32),
            pltpu.VMEM((1, beams), jnp.int32),
            pltpu.VMEM((2 * hop, 2 * window), jnp.bfloat16),
            pltpu.VMEM((2 * LANES, LANES), jnp.bfloat16),
            pltpu.VMEM((2 * LANES, padded), jnp.bfloat16),
            pltpu.VMEM((chans, total, LANES), jnp.bfloat16),
            pltpu.VMEM((wide, total, LANES), jnp.bfloat16),
            pltpu.VMEM((beams, width), jnp.float32),
            pltpu.VMEM((beams, width), jnp.float32),
            pltpu.VMEM((2 * beams, width), jnp.bfloat16),
            pltpu.VMEM((2 * beams, total // 2), jnp.float32),
            pltpu.VMEM((2 * beams, total // 2), jnp.bfloat16),
            pltpu.VMEM((beams, width), jnp.float32),
            pltpu.VMEM((8, width), jnp.float32),
            pltpu.VMEM((beams, total // 4), jnp.float32),
            pltpu.VMEM((chans, 8, LANES), jnp.float32),
            pltpu.VMEM((wide, 8, LANES), jnp.float32),
            pltpu.VMEM((wide, share, total // 4), jnp.bfloat16),
            pltpu.VMEM((chans, share, total // 4), jnp.bfloat16),
            pltpu.SemaphoreType.DMA((6,)),
            pltpu.SemaphoreType.DMA((parts,)),
            pltpu.SemaphoreType.DMA((parts,)),
            pltpu.SemaphoreType.DMA((1,)),
            pltpu.SemaphoreType.DMA((1,)),
            pltpu.SemaphoreType.DMA((1,)),
            pltpu.SemaphoreType.DMA((1,)),
        ],
        compiler_params=pltpu.CompilerParams(
            collective_id=0, has_side_effects=True, vmem_limit_bytes=64 * 2**20 - 2**16
        ),
    )(voltages, taps, flags.reshape(1, -1), positions, beam_index.reshape(1, -1))


def fits(voltages, taps, beam_index, wide):
    count, _, length = voltages.shape
    ntaps, chans = taps.shape
    total = length // chans - ntaps + 1
    return (
        2 * count == LANES
        and chans == wide
        and ROWS * chans == CHUNK
        and length % CHUNK < LANES
        and (ntaps - 1) * chans <= CHUNK
        and wide % 2 == 0
        and total % (16 * ROWS) == 0
        and beam_index.shape[0] % (ROWS * wide) == 0
        and (total // 4) % LANES == 0
    )


def local(voltages, taps, flags, positions, beam_index):
    if fits(voltages, taps, beam_index, lax.axis_size("wide")):
        return fused(voltages, taps, flags, positions, beam_index)
    return plain(voltages, taps, flags, positions, beam_index)


def solution(mesh):
    in_specs = (P(("grp", "wide"), None, None), P(), P(("grp", "wide")), P(), P("grp"))
    out_specs = P(("grp", "wide"), None, None)
    return jax.shard_map(local, mesh=mesh, in_specs=in_specs, out_specs=out_specs, check_vma=False)
```

```python
import functools
import math

import jax
import jax.numpy as jnp
import numpy as np
from jax import lax
from jax.experimental import pallas as pl
from jax.experimental.pallas import tpu as pltpu
from jax.sharding import PartitionSpec as P

ITERS = 2


damping = 0.5
grid_side = 32


def channelize(voltages, taps, flags):
    count = voltages.shape[0]
    chans = taps.shape[1]
    ntaps = taps.shape[0]
    total = voltages.shape[2] // chans - ntaps + 1
    samples = voltages.astype(jnp.float32).reshape(count, 2, total + ntaps - 1, chans)
    filtered = taps[0][None, None, None, :] * samples[:, :, 0:total, :]
    for tap in range(1, ntaps):
        filtered = filtered + taps[tap][None, None, None, :] * samples[:, :, tap : tap + total, :]
    branch = jnp.arange(chans, dtype=jnp.int32)
    angle = 2.0 * math.pi / chans * (branch[:, None] * branch[None, :] % chans).astype(jnp.float32)
    cosine = jnp.cos(angle)
    sine = jnp.sin(angle)
    high = lax.Precision.HIGHEST
    real_in = filtered[:, 0]
    imag_in = filtered[:, 1]
    real_out = jnp.einsum("asp,pc->acs", real_in, cosine, precision=high) + jnp.einsum(
        "asp,pc->acs", imag_in, sine, precision=high
    )
    imag_out = jnp.einsum("asp,pc->acs", imag_in, cosine, precision=high) - jnp.einsum(
        "asp,pc->acs", real_in, sine, precision=high
    )
    keep = flags.astype(jnp.float32)[:, None, None] / math.sqrt(chans)
    return jnp.stack([real_out * keep, imag_out * keep]).astype(jnp.bfloat16)


def steering(channel, positions, beam_index, chans):
    column = (beam_index % grid_side).astype(jnp.float32)
    row_cell = (beam_index // grid_side).astype(jnp.float32)
    east = (column + 0.5) / grid_side - 0.5
    north = (row_cell + 0.5) / grid_side - 0.5
    ratio = 1.0 + 0.5 * channel.astype(jnp.float32) / chans
    phase = (
        2.0
        * math.pi
        * ratio
        * (positions[0][:, None] * east[None, :] + positions[1][:, None] * north[None, :])
    )
    return (jnp.cos(phase), -jnp.sin(phase))


def form_beams(blocks, channel, positions, beam_index, total, chans):
    high = lax.Precision.HIGHEST
    cov_real = 0.0
    cov_imag = 0.0
    for block in blocks:
        left = jnp.concatenate([block[0], block[1]], axis=1)
        turned = jnp.concatenate([block[1], -block[0]], axis=1)
        cov_real = cov_real + jnp.dot(left, left.T, preferred_element_type=jnp.float32)
        cov_imag = cov_imag + jnp.dot(turned, left.T, preferred_element_type=jnp.float32)
    cov_real = cov_real / total
    cov_imag = cov_imag / total
    count = cov_real.shape[0]
    diagonal = jnp.diagonal(cov_real)
    loading = jnp.mean(diagonal) + 1e-05
    scaling = (damping / (diagonal + loading))[:, None]
    steer_real, steer_imag = steering(channel, positions, beam_index, chans)
    weight_real = scaling * steer_real
    weight_imag = scaling * steer_imag
    for sweep in range(ITERS):
        image_real = (
            jnp.dot(cov_real, weight_real, precision=high)
            - jnp.dot(cov_imag, weight_imag, precision=high)
            + loading * weight_real
        )
        image_imag = (
            jnp.dot(cov_real, weight_imag, precision=high)
            + jnp.dot(cov_imag, weight_real, precision=high)
            + loading * weight_imag
        )
        weight_real = weight_real + scaling * (steer_real - image_real)
        weight_imag = weight_imag + scaling * (steer_imag - image_imag)
    low_real = weight_real.astype(jnp.bfloat16)
    low_imag = weight_imag.astype(jnp.bfloat16)
    plain = jnp.concatenate([low_real, low_imag], axis=0)
    mixed = jnp.concatenate([low_real, -low_imag], axis=0)
    contract = (((0,), (0,)), ((), ()))
    reals = []
    imags = []
    for block in blocks:
        reals.append(
            lax.dot_general(
                plain,
                jnp.concatenate([block[0], block[1]], axis=0),
                contract,
                preferred_element_type=jnp.float32,
            )
        )
        imags.append(
            lax.dot_general(
                mixed,
                jnp.concatenate([block[1], block[0]], axis=0),
                contract,
                preferred_element_type=jnp.float32,
            )
        )
    norm_factor = 1.0 / math.sqrt(count)
    beams = (
        jnp.stack([jnp.concatenate(reals, axis=-1), jnp.concatenate(imags, axis=-1)]) * norm_factor
    )
    return beams.astype(jnp.bfloat16)


def detect(beams):
    floats = beams.astype(jnp.float32)
    energy = floats[:, 0] * floats[:, 0] + floats[:, 1] * floats[:, 1]
    shape = energy.shape
    return energy.reshape(shape[0], shape[1], shape[2] // 4, 4).sum(axis=-1)


def plain(voltages, taps, flags, positions, beam_index):
    spectra = channelize(voltages, taps, flags)
    chans = taps.shape[1]
    per_dev = chans // lax.axis_size("wide")
    first = lax.axis_index("wide") * per_dev
    total = spectra.shape[3]
    pieces = [lax.all_to_all(spectra, "wide", split_axis=2, concat_axis=1, tiled=True)]
    stacked = [jnp.moveaxis(piece, 2, 0) for piece in pieces]

    def one_channel(operands):
        offset, blocks = operands
        return form_beams(blocks, first + offset, positions, beam_index, total, chans)

    beams = lax.map(one_channel, (jnp.arange(per_dev, dtype=jnp.int32), stacked))
    result = lax.all_to_all(
        detect(beams).astype(jnp.bfloat16), "wide", split_axis=1, concat_axis=0, tiled=True
    ).astype(jnp.float32)
    return jnp.transpose(result, (1, 0, 2))


MESH = pl.DeviceIdType.MESH
LANES = 128
ROWS = 16
NT = (((1,), (1,)), ((), ()))


def cosine_turns(turns):
    frac = jnp.abs(turns - jnp.floor(turns + 0.5))
    x = (0.25 - frac) * (2.0 * math.pi)
    sq = x * x
    poly = -1.0 / 39916800.0
    for term in (1.0 / 362880.0, -1.0 / 5040.0, 1.0 / 120.0, -1.0 / 6.0, 1.0):
        poly = poly * sq + term
    return x * poly


def swap_halves(block):
    return pltpu.roll(block, LANES // 2, 1)


def kernel(
    volt_hbm, taps_hbm, flags_hbm, place_hbm, index_hbm, out_ref,
    volt, taps_ref, flags_ref, place_ref, index_ref, bank, mixed, sent, spec, steer, weight, low, image, applied, scale,
    tell, told, give, got,
    volt_sem, send_sem, recv_sem, tell_sem, told_sem, give_sem, got_sem,
    *, wide, total, chans, window, bounds, early,
):
    me = lax.axis_index("wide")
    parts = len(bounds) - 1
    beams = index_hbm.shape[1]
    width = wide * LANES
    hop = ROWS * chans
    length = volt_hbm.shape[1]
    ntaps = taps_hbm.shape[0]
    half_lanes = LANES // 2

    barrier = pltpu.get_barrier_semaphore()
    first_reach = bounds[1] * chans + window - hop
    loads = [
        pltpu.make_async_copy(source, target, volt_sem.at[at])
        for at, (source, target) in enumerate(
            [
                (taps_hbm, taps_ref),
                (flags_hbm, flags_ref),
                (place_hbm, place_ref),
                (index_hbm, index_ref),
                (volt_hbm.at[:, :first_reach], volt.at[:, :first_reach]),
                (volt_hbm.at[:, first_reach:], volt.at[:, first_reach:]),
            ]
        )
    ]
    for load in loads:
        load.start()

    def greet(off, carry):
        pl.semaphore_signal(
            barrier, inc=1, device_id={"wide": lax.rem(me + off, wide)}, device_id_type=MESH
        )
        return carry

    lax.fori_loop(1, wide, greet, 0)

    ranked = sorted(range(1, wide), key=lambda off: (abs(off - wide // 2), off))
    cut = (len(ranked) + 1) // 2
    mixed_order = [
        entry for duo in zip(ranked[:cut], ranked[cut:] + [None]) for entry in duo
    ]
    mixed_order = [entry for entry in mixed_order if entry is not None]
    turned_order = list(mixed_order)
    for at in range(0, len(turned_order) - 1, 2):
        turned_order[at], turned_order[at + 1] = turned_order[at + 1], turned_order[at]

    def everyone(act):
        core = lax.rem(me, 2)
        for one, two in zip(mixed_order, turned_order):
            act(lax.rem(me + (one + core * (two - one)), wide))

    def iota(shape, axis):
        return lax.broadcasted_iota(jnp.int32, shape, axis)

    for load in loads[:4]:
        load.wait()
    slot = iota((ROWS, window), 1) // chans
    delay = slot - iota((ROWS, window), 0)
    spread = jnp.where(iota((chans, window), 1) % chans == iota((chans, window), 0), 1.0, 0.0)
    tiled = jnp.dot(
        taps_ref[...], spread, precision=lax.Precision.HIGHEST, preferred_element_type=jnp.float32
    )
    filt = jnp.zeros((ROWS, window), jnp.float32)
    for tap in range(ntaps):
        filt = filt + jnp.where(delay == tap, tiled[tap : tap + 1, :], 0.0)
    spin = (iota((chans, window), 0) * (iota((chans, window), 1) % chans)) % chans
    spin = spin.astype(jnp.float32) / chans
    for half in range(2):
        wave = cosine_turns(spin - 0.25 * half) / math.sqrt(chans)
        for channel in range(chans):
            entry = wave[channel : channel + 1, :] * filt
            top = entry.astype(jnp.bfloat16)
            rest = (entry - top.astype(jnp.float32)).astype(jnp.bfloat16)
            cols = slice(half * window, (half + 1) * window)
            bank[channel * ROWS : (channel + 1) * ROWS, cols] = top
            bank[hop + channel * ROWS : hop + (channel + 1) * ROWS, cols] = rest

    doubled = jnp.where(iota((half_lanes, LANES), 1) // 2 == iota((half_lanes, LANES), 0), 1.0, 0.0)
    keep = jnp.broadcast_to(flags_ref[...].astype(jnp.float32), (8, half_lanes))
    keep = jnp.dot(
        keep.astype(jnp.bfloat16), doubled.astype(jnp.bfloat16), preferred_element_type=jnp.float32
    )[0:1]
    row = iota((2 * LANES, LANES), 0)
    antenna = row % half_lanes
    quarter = row // half_lanes
    from_part = jnp.where((quarter == 1) | (quarter == 2), 1, 0)
    chosen = iota((2 * LANES, LANES), 1) == 2 * antenna + from_part
    order = jnp.where(chosen, jnp.where(quarter == 3, -keep, keep), 0.0).astype(jnp.bfloat16)

    def mix(start, size):
        block = volt[:, start : start + size]
        mixed[:, start : start + size] = jnp.dot(
            order, block, preferred_element_type=jnp.float32
        ).astype(jnp.bfloat16)

    def rows_of(part):
        return slice(bounds[part], bounds[part + 1])

    def lanes_of(block):
        return pl.ds(pl.multiple_of(block * LANES, LANES), LANES)

    def remote(source, target, out_sem, in_sem, other):
        return pltpu.make_async_remote_copy(
            src_ref=source,
            dst_ref=target,
            send_sem=out_sem,
            recv_sem=in_sem,
            device_id={"wide": other},
            device_id_type=MESH,
        )

    def await_bytes(ref, sem):
        pltpu.make_async_copy(ref, ref, sem).wait()

    def ship(part):
        rows = rows_of(part)
        everyone(
            lambda other: remote(
                sent.at[other, rows, :], spec.at[me, rows, :],
                send_sem.at[part], recv_sem.at[part], other,
            ).start()
        )
        pltpu.make_async_copy(
            sent.at[me, rows, :], spec.at[me, rows, :], recv_sem.at[part]
        ).start()

    tell[...] = jnp.zeros_like(tell)

    def channelize_pair(pair, carry):
        start = pl.multiple_of(pair * (2 * hop), LANES)
        both = jnp.concatenate(
            [
                jnp.concatenate(
                    [mixed[:LANES, pl.ds(at, window)], mixed[LANES:, pl.ds(at, window)]], axis=1
                )
                for at in (start, pl.multiple_of(start + hop, LANES))
            ],
            axis=0,
        )
        acc = lax.dot_general(bank[...], both, NT, preferred_element_type=jnp.float32)
        rounded = (acc[:hop] + acc[hop:]).astype(jnp.bfloat16)
        for side in range(2):
            at = pl.multiple_of(pair * (2 * ROWS) + side * ROWS, ROWS)
            block = rounded[:, side * LANES : (side + 1) * LANES].reshape(chans, ROWS, LANES)
            sent[:, pl.ds(at, ROWS), :] = block
            block = block.astype(jnp.float32)
            block = block * block
            tell[...] += block[:, :8] + block[:, 8:]
        return carry

    loads[4].wait()
    tail = length // LANES * LANES
    mixed[:, tail:] = jnp.zeros((2 * LANES, mixed.shape[1] - tail), jnp.bfloat16)
    over = window - hop
    reach = 0
    for part in range(parts):
        if part == 1:
            loads[5].wait()
        upto = min(bounds[part + 1] * chans + over, length)
        mix(reach, upto - reach)
        reach = upto
        span = 2 * ROWS
        lax.fori_loop(bounds[part] // span, bounds[part + 1] // span, channelize_pair, 0)
        if part == 0:
            pl.semaphore_wait(barrier, wide - 1)
        if part < early:
            ship(part)
    everyone(
        lambda other: remote(
            tell.at[other], told.at[me], tell_sem.at[0], told_sem.at[0], other
        ).start()
    )
    pltpu.make_async_copy(tell.at[me], told.at[me], told_sem.at[0]).start()
    for part in range(early, parts):
        ship(part)

    index = index_ref[...]
    ratio = 1.0 + 0.5 * me.astype(jnp.float32) / chans
    cells = [
        ((index % grid_side).astype(jnp.float32) + 0.5) / grid_side - 0.5,
        ((index // grid_side).astype(jnp.float32) + 0.5) / grid_side - 0.5,
    ]
    same = iota((beams, beams), 0) == iota((beams, beams), 1)
    east, north = [
        jnp.sum(jnp.where(same, cell, 0.0), axis=1, keepdims=True) * ratio for cell in cells
    ]
    first_half = iota((1, LANES), 1) < half_lanes
    turn = jnp.where(first_half, 0.0, 0.25)

    def steer_duo(duo, carry):
        here = place_ref[:, lanes_of(duo)]
        here = jnp.concatenate([here, jnp.zeros((6, LANES), jnp.float32)], axis=0)
        there = swap_halves(here)
        for side in range(2):
            both = jnp.where(first_half, here, there) if side == 0 else jnp.where(
                first_half, there, here
            )
            turns = east * both[0:1] + north * both[1:2] + turn
            steer[:, lanes_of(2 * duo + side)] = cosine_turns(turns)
        return carry

    lax.fori_loop(0, wide // 2, steer_duo, 0)

    await_bytes(told, told_sem.at[0])
    sign = jnp.where(first_half, 1.0, -1.0)
    power = jnp.sum(told[...], axis=1, keepdims=True) * (1.0 / total)
    loading = jnp.sum(power) / (width // 2) + 1e-05
    for block in range(wide):
        piece = jnp.broadcast_to(power[block], (8, LANES))
        piece = piece + swap_halves(piece)
        scale[:, block * LANES : (block + 1) * LANES] = 0.5 / (piece + loading)

    def keep_low(lanes, value):
        low[:beams, lanes] = value.astype(jnp.bfloat16)
        low[beams:, lanes] = (swap_halves(value) * sign).astype(jnp.bfloat16)

    def first_block(block, carry):
        lanes = lanes_of(block)
        value = scale[0:1, lanes] * steer[:, lanes]
        weight[:, lanes] = value
        keep_low(lanes, value)
        return carry

    lax.fori_loop(0, wide, first_block, 0)

    def project(rows):
        strip = jnp.concatenate([spec[block, rows, :] for block in range(wide)], axis=1)
        return lax.dot_general(low[...], strip, NT, preferred_element_type=jnp.float32)

    def back_project(rows, last, sweep, first):
        def duo_block(duo, carry):
            strip = jnp.concatenate([spec[2 * duo, rows, :], spec[2 * duo + 1, rows, :]], axis=1)
            back = jnp.dot(image[:, rows], strip, preferred_element_type=jnp.float32)
            for side in range(2):
                lanes = lanes_of(2 * duo + side)
                cols = slice(side * LANES, (side + 1) * LANES)
                fresh = back[:beams, cols] - sign * swap_halves(back[beams:, cols])
                if not first:
                    fresh = applied[:, lanes] + fresh
                if not last:
                    applied[:, lanes] = fresh
                    continue
                value = weight[:, lanes]
                value = value + scale[0:1, lanes] * (
                    steer[:, lanes] - (fresh * (1.0 / total) + loading * value)
                )
                if sweep < ITERS - 1:
                    weight[:, lanes] = value
                keep_low(lanes, value)
            return carry

        lax.fori_loop(0, wide // 2, duo_block, 0)

    for part in range(parts):
        rows = rows_of(part)
        await_bytes(spec.at[:, rows, :], recv_sem.at[part])
        if bounds[part + 1] % (total // 2):
            continue
        rows = slice(bounds[part + 1] - total // 2, bounds[part + 1])
        image[:, rows] = project(rows).astype(jnp.bfloat16)
        back_project(rows, part + 1 == parts, 0, rows.start == 0)

    half_rows = total // 2
    halves = [slice(half * half_rows, (half + 1) * half_rows) for half in range(2)]
    for sweep in range(1, ITERS):
        for rows in halves:
            image[:, rows] = project(rows).astype(jnp.bfloat16)
        back_project(slice(0, total), True, sweep, True)

    group = total // 4
    share = give.shape[1]
    sums = jnp.zeros((beams, group), jnp.float32)
    for half, rows in enumerate(halves):
        value = project(rows)
        energy = value[:beams] * value[:beams] + value[beams:] * value[beams:]
        energy = energy * (2.0 / width)
        top = energy.astype(jnp.bfloat16)
        rest = (energy - top.astype(jnp.float32)).astype(jnp.bfloat16)
        source = iota((half_rows, group), 0) + half * half_rows
        target = iota((half_rows, group), 1) * 4
        pick = jnp.where((source >= target) & (source < target + 4), 1.0, 0.0)
        pick = pick.astype(jnp.bfloat16)
        sums = sums + jnp.dot(top, pick, preferred_element_type=jnp.float32)
        sums = sums + jnp.dot(rest, pick, preferred_element_type=jnp.float32)
    give[...] = sums.astype(jnp.bfloat16).reshape(wide, share, group)
    everyone(
        lambda other: remote(
            give.at[other], got.at[me], give_sem.at[0], got_sem.at[0], other
        ).start()
    )
    pltpu.make_async_copy(give.at[me], got.at[me], got_sem.at[0]).start()
    for part in range(parts):
        await_bytes(sent.at[: wide - 1, rows_of(part), :], send_sem.at[part])
    await_bytes(tell.at[: wide - 1], tell_sem.at[0])
    await_bytes(got, got_sem.at[0])
    for channel in range(chans):
        out_ref[:, channel, :] = got[channel].astype(jnp.float32)
    await_bytes(give.at[: wide - 1], give_sem.at[0])


def fused(voltages, taps, flags, positions, beam_index):
    wide = lax.axis_size("wide")
    count, _, length = voltages.shape
    ntaps, chans = taps.shape
    total = length // chans - ntaps + 1
    beams = beam_index.shape[0]
    hop = ROWS * chans
    window = -(-(ROWS + ntaps - 1) * chans // LANES) * LANES
    padded = (total // ROWS - 1) * hop + window
    bounds = [0, LANES // 2] + list(range(LANES, total + 1, LANES))
    parts = len(bounds) - 1
    share = beams // wide
    width = wide * LANES
    vmem = pl.BlockSpec(memory_space=pltpu.VMEM)
    return pl.pallas_call(
        functools.partial(
            kernel, wide=wide, total=total, chans=chans, window=window, bounds=bounds,
            early=min(3, parts),
        ),
        out_shape=jax.ShapeDtypeStruct((share, chans, total // 4), jnp.float32),
        in_specs=[pl.BlockSpec(memory_space=pl.ANY)] * 5,
        out_specs=vmem,
        scratch_shapes=[
            pltpu.VMEM((2 * count, length), jnp.bfloat16),
            pltpu.VMEM(taps.shape, jnp.float32),
            pltpu.VMEM((1, count), jnp.int32),
            pltpu.VMEM(positions.shape, jnp.float32),
            pltpu.VMEM((1, beams), jnp.int32),
            pltpu.VMEM((2 * hop, 2 * window), jnp.bfloat16),
            pltpu.VMEM((2 * LANES, padded), jnp.bfloat16),
            pltpu.VMEM((chans, total, LANES), jnp.bfloat16),
            pltpu.VMEM((wide, total, LANES), jnp.bfloat16),
            pltpu.VMEM((beams, width), jnp.float32),
            pltpu.VMEM((beams, width), jnp.float32),
            pltpu.VMEM((2 * beams, width), jnp.bfloat16),
            pltpu.VMEM((2 * beams, total), jnp.bfloat16),
            pltpu.VMEM((beams, width), jnp.float32),
            pltpu.VMEM((8, width), jnp.float32),
            pltpu.VMEM((chans, 8, LANES), jnp.float32),
            pltpu.VMEM((wide, 8, LANES), jnp.float32),
            pltpu.VMEM((wide, share, total // 4), jnp.bfloat16),
            pltpu.VMEM((chans, share, total // 4), jnp.bfloat16),
            pltpu.SemaphoreType.DMA((6,)),
            pltpu.SemaphoreType.DMA((parts,)),
            pltpu.SemaphoreType.DMA((parts,)),
            pltpu.SemaphoreType.DMA((1,)),
            pltpu.SemaphoreType.DMA((1,)),
            pltpu.SemaphoreType.DMA((1,)),
            pltpu.SemaphoreType.DMA((1,)),
        ],
        compiler_params=pltpu.CompilerParams(
            collective_id=0, has_side_effects=True, vmem_limit_bytes=64 * 2**20 - 2**16
        ),
    )(voltages.reshape(2 * count, length), taps, flags.reshape(1, -1), positions, beam_index.reshape(1, -1))


def fits(voltages, taps, beam_index, wide):
    count, _, length = voltages.shape
    ntaps, chans = taps.shape
    total = length // chans - ntaps + 1
    return (
        2 * count == LANES
        and chans == wide
        and (ROWS * chans) % LANES == 0
        and wide % 2 == 0
        and total % 256 == 0
        and beam_index.shape[0] % (ROWS * wide) == 0
        and (total // 4) % LANES == 0
    )


def local(voltages, taps, flags, positions, beam_index):
    if fits(voltages, taps, beam_index, lax.axis_size("wide")):
        return fused(voltages, taps, flags, positions, beam_index)
    return plain(voltages, taps, flags, positions, beam_index)


def solution(mesh):
    in_specs = (P(("grp", "wide"), None, None), P(), P(("grp", "wide")), P(), P("grp"))
    out_specs = P(("grp", "wide"), None, None)
    return jax.shard_map(local, mesh=mesh, in_specs=in_specs, out_specs=out_specs, check_vma=False)
```

```python
import functools
import math

import jax
import jax.numpy as jnp
import numpy as np
from jax import lax
from jax.experimental import pallas as pl
from jax.experimental.pallas import tpu as pltpu
from jax.sharding import PartitionSpec as P

ITERS = 2


damping = 0.5
grid_side = 32


def channelize(voltages, taps, flags):
    count = voltages.shape[0]
    chans = taps.shape[1]
    ntaps = taps.shape[0]
    total = voltages.shape[2] // chans - ntaps + 1
    samples = voltages.astype(jnp.float32).reshape(count, 2, total + ntaps - 1, chans)
    filtered = taps[0][None, None, None, :] * samples[:, :, 0:total, :]
    for tap in range(1, ntaps):
        filtered = filtered + taps[tap][None, None, None, :] * samples[:, :, tap : tap + total, :]
    branch = jnp.arange(chans, dtype=jnp.int32)
    angle = 2.0 * math.pi / chans * (branch[:, None] * branch[None, :] % chans).astype(jnp.float32)
    cosine = jnp.cos(angle)
    sine = jnp.sin(angle)
    high = lax.Precision.HIGHEST
    real_in = filtered[:, 0]
    imag_in = filtered[:, 1]
    real_out = jnp.einsum("asp,pc->acs", real_in, cosine, precision=high) + jnp.einsum(
        "asp,pc->acs", imag_in, sine, precision=high
    )
    imag_out = jnp.einsum("asp,pc->acs", imag_in, cosine, precision=high) - jnp.einsum(
        "asp,pc->acs", real_in, sine, precision=high
    )
    keep = flags.astype(jnp.float32)[:, None, None] / math.sqrt(chans)
    return jnp.stack([real_out * keep, imag_out * keep]).astype(jnp.bfloat16)


def steering(channel, positions, beam_index, chans):
    column = (beam_index % grid_side).astype(jnp.float32)
    row_cell = (beam_index // grid_side).astype(jnp.float32)
    east = (column + 0.5) / grid_side - 0.5
    north = (row_cell + 0.5) / grid_side - 0.5
    ratio = 1.0 + 0.5 * channel.astype(jnp.float32) / chans
    phase = (
        2.0
        * math.pi
        * ratio
        * (positions[0][:, None] * east[None, :] + positions[1][:, None] * north[None, :])
    )
    return (jnp.cos(phase), -jnp.sin(phase))


def form_beams(blocks, channel, positions, beam_index, total, chans):
    high = lax.Precision.HIGHEST
    cov_real = 0.0
    cov_imag = 0.0
    for block in blocks:
        left = jnp.concatenate([block[0], block[1]], axis=1)
        turned = jnp.concatenate([block[1], -block[0]], axis=1)
        cov_real = cov_real + jnp.dot(left, left.T, preferred_element_type=jnp.float32)
        cov_imag = cov_imag + jnp.dot(turned, left.T, preferred_element_type=jnp.float32)
    cov_real = cov_real / total
    cov_imag = cov_imag / total
    count = cov_real.shape[0]
    diagonal = jnp.diagonal(cov_real)
    loading = jnp.mean(diagonal) + 1e-05
    scaling = (damping / (diagonal + loading))[:, None]
    steer_real, steer_imag = steering(channel, positions, beam_index, chans)
    weight_real = scaling * steer_real
    weight_imag = scaling * steer_imag
    for sweep in range(ITERS):
        image_real = (
            jnp.dot(cov_real, weight_real, precision=high)
            - jnp.dot(cov_imag, weight_imag, precision=high)
            + loading * weight_real
        )
        image_imag = (
            jnp.dot(cov_real, weight_imag, precision=high)
            + jnp.dot(cov_imag, weight_real, precision=high)
            + loading * weight_imag
        )
        weight_real = weight_real + scaling * (steer_real - image_real)
        weight_imag = weight_imag + scaling * (steer_imag - image_imag)
    low_real = weight_real.astype(jnp.bfloat16)
    low_imag = weight_imag.astype(jnp.bfloat16)
    plain = jnp.concatenate([low_real, low_imag], axis=0)
    mixed = jnp.concatenate([low_real, -low_imag], axis=0)
    contract = (((0,), (0,)), ((), ()))
    reals = []
    imags = []
    for block in blocks:
        reals.append(
            lax.dot_general(
                plain,
                jnp.concatenate([block[0], block[1]], axis=0),
                contract,
                preferred_element_type=jnp.float32,
            )
        )
        imags.append(
            lax.dot_general(
                mixed,
                jnp.concatenate([block[1], block[0]], axis=0),
                contract,
                preferred_element_type=jnp.float32,
            )
        )
    norm_factor = 1.0 / math.sqrt(count)
    beams = (
        jnp.stack([jnp.concatenate(reals, axis=-1), jnp.concatenate(imags, axis=-1)]) * norm_factor
    )
    return beams.astype(jnp.bfloat16)


def detect(beams):
    floats = beams.astype(jnp.float32)
    energy = floats[:, 0] * floats[:, 0] + floats[:, 1] * floats[:, 1]
    shape = energy.shape
    return energy.reshape(shape[0], shape[1], shape[2] // 4, 4).sum(axis=-1)


def plain(voltages, taps, flags, positions, beam_index):
    spectra = channelize(voltages, taps, flags)
    chans = taps.shape[1]
    per_dev = chans // lax.axis_size("wide")
    first = lax.axis_index("wide") * per_dev
    total = spectra.shape[3]
    pieces = [lax.all_to_all(spectra, "wide", split_axis=2, concat_axis=1, tiled=True)]
    stacked = [jnp.moveaxis(piece, 2, 0) for piece in pieces]

    def one_channel(operands):
        offset, blocks = operands
        return form_beams(blocks, first + offset, positions, beam_index, total, chans)

    beams = lax.map(one_channel, (jnp.arange(per_dev, dtype=jnp.int32), stacked))
    result = lax.all_to_all(
        detect(beams).astype(jnp.bfloat16), "wide", split_axis=1, concat_axis=0, tiled=True
    ).astype(jnp.float32)
    return jnp.transpose(result, (1, 0, 2))


MESH = pl.DeviceIdType.MESH
LANES = 128
ROWS = 16
NT = (((1,), (1,)), ((), ()))


def cosine_turns(turns):
    frac = jnp.abs(turns - jnp.floor(turns + 0.5))
    x = (0.25 - frac) * (2.0 * math.pi)
    sq = x * x
    poly = -1.0 / 39916800.0
    for term in (1.0 / 362880.0, -1.0 / 5040.0, 1.0 / 120.0, -1.0 / 6.0, 1.0):
        poly = poly * sq + term
    return x * poly


def swap_halves(block):
    return pltpu.roll(block, LANES // 2, 1)


def kernel(
    volt_hbm, taps_hbm, flags_hbm, place_hbm, index_hbm, out_ref,
    volt, taps_ref, flags_ref, place_ref, index_ref, bank, mixed, sent, spec, steer, weight, low, image, applied, scale,
    tell, told, give, got,
    volt_sem, send_sem, recv_sem, tell_sem, told_sem, give_sem, got_sem,
    *, wide, total, chans, window, bounds, early,
):
    me = lax.axis_index("wide")
    parts = len(bounds) - 1
    beams = index_hbm.shape[1]
    width = wide * LANES
    hop = ROWS * chans
    length = volt_hbm.shape[2]
    ntaps = taps_hbm.shape[0]
    half_lanes = LANES // 2

    barrier = pltpu.get_barrier_semaphore()
    first_reach = bounds[1] * chans + window - hop
    loads = [
        pltpu.make_async_copy(source, target, volt_sem.at[at])
        for at, (source, target) in enumerate(
            [
                (taps_hbm, taps_ref),
                (flags_hbm, flags_ref),
                (place_hbm, place_ref),
                (index_hbm, index_ref),
                (volt_hbm.at[:, :, :first_reach], volt.at[:, :, :first_reach]),
                (volt_hbm.at[:, :, first_reach:], volt.at[:, :, first_reach:]),
            ]
        )
    ]
    for load in loads:
        load.start()

    def greet(off, carry):
        pl.semaphore_signal(
            barrier, inc=1, device_id={"wide": lax.rem(me + off, wide)}, device_id_type=MESH
        )
        return carry

    lax.fori_loop(1, wide, greet, 0)

    ranked = sorted(range(1, wide), key=lambda off: (abs(off - wide // 2), off))
    cut = (len(ranked) + 1) // 2
    mixed_order = [
        entry for duo in zip(ranked[:cut], ranked[cut:] + [None]) for entry in duo
    ]
    mixed_order = [entry for entry in mixed_order if entry is not None]
    turned_order = list(mixed_order)
    for at in range(0, len(turned_order) - 1, 2):
        turned_order[at], turned_order[at + 1] = turned_order[at + 1], turned_order[at]

    def everyone(act):
        core = lax.rem(me, 2)
        for one, two in zip(mixed_order, turned_order):
            act(lax.rem(me + (one + core * (two - one)), wide))

    def iota(shape, axis):
        return lax.broadcasted_iota(jnp.int32, shape, axis)

    for load in loads[:4]:
        load.wait()
    slot = iota((ROWS, window), 1) // chans
    delay = slot - iota((ROWS, window), 0)
    spread = jnp.where(iota((chans, window), 1) % chans == iota((chans, window), 0), 1.0, 0.0)
    tiled = jnp.dot(
        taps_ref[...], spread, precision=lax.Precision.HIGHEST, preferred_element_type=jnp.float32
    )
    filt = jnp.zeros((ROWS, window), jnp.float32)
    for tap in range(ntaps):
        filt = filt + jnp.where(delay == tap, tiled[tap : tap + 1, :], 0.0)
    spin = (iota((chans, window), 0) * (iota((chans, window), 1) % chans)) % chans
    spin = spin.astype(jnp.float32) / chans
    for half in range(2):
        wave = cosine_turns(spin - 0.25 * half) / math.sqrt(chans)
        for channel in range(chans):
            entry = wave[channel : channel + 1, :] * filt
            top = entry.astype(jnp.bfloat16)
            rest = (entry - top.astype(jnp.float32)).astype(jnp.bfloat16)
            cols = slice(half * window, (half + 1) * window)
            bank[channel * ROWS : (channel + 1) * ROWS, cols] = top
            bank[hop + channel * ROWS : hop + (channel + 1) * ROWS, cols] = rest

    doubled = jnp.where(iota((half_lanes, LANES), 1) // 2 == iota((half_lanes, LANES), 0), 1.0, 0.0)
    keep = jnp.broadcast_to(flags_ref[...].astype(jnp.float32), (8, half_lanes))
    keep = jnp.dot(
        keep.astype(jnp.bfloat16), doubled.astype(jnp.bfloat16), preferred_element_type=jnp.float32
    )[0:1]
    row = iota((2 * LANES, LANES), 0)
    antenna = row % half_lanes
    quarter = row // half_lanes
    from_part = jnp.where((quarter == 1) | (quarter == 2), 1, 0)
    chosen = iota((2 * LANES, LANES), 1) == 2 * antenna + from_part
    order = jnp.where(chosen, jnp.where(quarter == 3, -keep, keep), 0.0).astype(jnp.bfloat16)

    def mix(start, size):
        block = volt[:, :, start : start + size].reshape(LANES, size)
        mixed[:, start : start + size] = jnp.dot(
            order, block, preferred_element_type=jnp.float32
        ).astype(jnp.bfloat16)

    def rows_of(part):
        return slice(bounds[part], bounds[part + 1])

    def lanes_of(block):
        return pl.ds(pl.multiple_of(block * LANES, LANES), LANES)

    def remote(source, target, out_sem, in_sem, other):
        return pltpu.make_async_remote_copy(
            src_ref=source,
            dst_ref=target,
            send_sem=out_sem,
            recv_sem=in_sem,
            device_id={"wide": other},
            device_id_type=MESH,
        )

    def await_bytes(ref, sem):
        pltpu.make_async_copy(ref, ref, sem).wait()

    def ship(part):
        rows = rows_of(part)
        everyone(
            lambda other: remote(
                sent.at[other, rows, :], spec.at[me, rows, :],
                send_sem.at[part], recv_sem.at[part], other,
            ).start()
        )
        pltpu.make_async_copy(
            sent.at[me, rows, :], spec.at[me, rows, :], recv_sem.at[part]
        ).start()

    tell[...] = jnp.zeros_like(tell)

    def channelize_pair(pair, carry):
        start = pl.multiple_of(pair * (2 * hop), LANES)
        both = jnp.concatenate(
            [
                jnp.concatenate(
                    [mixed[:LANES, pl.ds(at, window)], mixed[LANES:, pl.ds(at, window)]], axis=1
                )
                for at in (start, pl.multiple_of(start + hop, LANES))
            ],
            axis=0,
        )
        acc = lax.dot_general(bank[...], both, NT, preferred_element_type=jnp.float32)
        rounded = (acc[:hop] + acc[hop:]).astype(jnp.bfloat16)
        for side in range(2):
            at = pl.multiple_of(pair * (2 * ROWS) + side * ROWS, ROWS)
            block = rounded[:, side * LANES : (side + 1) * LANES].reshape(chans, ROWS, LANES)
            sent[:, pl.ds(at, ROWS), :] = block
            block = block.astype(jnp.float32)
            block = block * block
            tell[...] += block[:, :8] + block[:, 8:]
        return carry

    loads[4].wait()
    tail = length // LANES * LANES
    mixed[:, tail:] = jnp.zeros((2 * LANES, mixed.shape[1] - tail), jnp.bfloat16)
    over = window - hop
    reach = 0
    for part in range(parts):
        if part == 1:
            loads[5].wait()
        upto = min(bounds[part + 1] * chans + over, length)
        mix(reach, upto - reach)
        reach = upto
        span = 2 * ROWS
        lax.fori_loop(bounds[part] // span, bounds[part + 1] // span, channelize_pair, 0)
        if part == 0:
            pl.semaphore_wait(barrier, wide - 1)
        if part < early:
            ship(part)
    everyone(
        lambda other: remote(
            tell.at[other], told.at[me], tell_sem.at[0], told_sem.at[0], other
        ).start()
    )
    pltpu.make_async_copy(tell.at[me], told.at[me], told_sem.at[0]).start()
    for part in range(early, parts):
        ship(part)

    index = index_ref[...]
    ratio = 1.0 + 0.5 * me.astype(jnp.float32) / chans
    cells = [
        ((index % grid_side).astype(jnp.float32) + 0.5) / grid_side - 0.5,
        ((index // grid_side).astype(jnp.float32) + 0.5) / grid_side - 0.5,
    ]
    same = iota((beams, beams), 0) == iota((beams, beams), 1)
    east, north = [
        jnp.sum(jnp.where(same, cell, 0.0), axis=1, keepdims=True) * ratio for cell in cells
    ]
    first_half = iota((1, LANES), 1) < half_lanes
    turn = jnp.where(first_half, 0.0, 0.25)

    def steer_duo(duo, carry):
        here = place_ref[:, lanes_of(duo)]
        here = jnp.concatenate([here, jnp.zeros((6, LANES), jnp.float32)], axis=0)
        there = swap_halves(here)
        for side in range(2):
            both = jnp.where(first_half, here, there) if side == 0 else jnp.where(
                first_half, there, here
            )
            turns = east * both[0:1] + north * both[1:2] + turn
            steer[:, lanes_of(2 * duo + side)] = cosine_turns(turns)
        return carry

    lax.fori_loop(0, wide // 2, steer_duo, 0)

    await_bytes(told, told_sem.at[0])
    sign = jnp.where(first_half, 1.0, -1.0)
    power = jnp.sum(told[...], axis=1, keepdims=True) * (1.0 / total)
    loading = jnp.sum(power) / (width // 2) + 1e-05
    for block in range(wide):
        piece = jnp.broadcast_to(power[block], (8, LANES))
        piece = piece + swap_halves(piece)
        scale[:, block * LANES : (block + 1) * LANES] = 0.5 / (piece + loading)

    def keep_low(lanes, value):
        low[:beams, lanes] = value.astype(jnp.bfloat16)
        low[beams:, lanes] = (swap_halves(value) * sign).astype(jnp.bfloat16)

    def first_block(block, carry):
        lanes = lanes_of(block)
        value = scale[0:1, lanes] * steer[:, lanes]
        weight[:, lanes] = value
        keep_low(lanes, value)
        return carry

    lax.fori_loop(0, wide, first_block, 0)

    def project(rows):
        strip = jnp.concatenate([spec[block, rows, :] for block in range(wide)], axis=1)
        return lax.dot_general(low[...], strip, NT, preferred_element_type=jnp.float32)

    def back_project(rows, last, sweep, first):
        def duo_block(duo, carry):
            strip = jnp.concatenate([spec[2 * duo, rows, :], spec[2 * duo + 1, rows, :]], axis=1)
            back = jnp.dot(image[:, rows], strip, preferred_element_type=jnp.float32)
            for side in range(2):
                lanes = lanes_of(2 * duo + side)
                cols = slice(side * LANES, (side + 1) * LANES)
                fresh = back[:beams, cols] - sign * swap_halves(back[beams:, cols])
                if not first:
                    fresh = applied[:, lanes] + fresh
                if not last:
                    applied[:, lanes] = fresh
                    continue
                value = weight[:, lanes]
                value = value + scale[0:1, lanes] * (
                    steer[:, lanes] - (fresh * (1.0 / total) + loading * value)
                )
                if sweep < ITERS - 1:
                    weight[:, lanes] = value
                keep_low(lanes, value)
            return carry

        lax.fori_loop(0, wide // 2, duo_block, 0)

    for part in range(parts):
        rows = rows_of(part)
        await_bytes(spec.at[:, rows, :], recv_sem.at[part])
        if bounds[part + 1] % (total // 2):
            continue
        rows = slice(bounds[part + 1] - total // 2, bounds[part + 1])
        image[:, rows] = project(rows).astype(jnp.bfloat16)
        back_project(rows, part + 1 == parts, 0, rows.start == 0)

    half_rows = total // 2
    halves = [slice(half * half_rows, (half + 1) * half_rows) for half in range(2)]
    for sweep in range(1, ITERS):
        for rows in halves:
            image[:, rows] = project(rows).astype(jnp.bfloat16)
        back_project(slice(0, total), True, sweep, True)

    group = total // 4
    share = give.shape[1]
    sums = jnp.zeros((beams, group), jnp.float32)
    for half, rows in enumerate(halves):
        value = project(rows)
        energy = value[:beams] * value[:beams] + value[beams:] * value[beams:]
        energy = energy * (2.0 / width)
        top = energy.astype(jnp.bfloat16)
        rest = (energy - top.astype(jnp.float32)).astype(jnp.bfloat16)
        source = iota((half_rows, group), 0) + half * half_rows
        target = iota((half_rows, group), 1) * 4
        pick = jnp.where((source >= target) & (source < target + 4), 1.0, 0.0)
        pick = pick.astype(jnp.bfloat16)
        sums = sums + jnp.dot(top, pick, preferred_element_type=jnp.float32)
        sums = sums + jnp.dot(rest, pick, preferred_element_type=jnp.float32)
    give[...] = sums.astype(jnp.bfloat16).reshape(wide, share, group)
    everyone(
        lambda other: remote(
            give.at[other], got.at[me], give_sem.at[0], got_sem.at[0], other
        ).start()
    )
    pltpu.make_async_copy(give.at[me], got.at[me], got_sem.at[0]).start()
    for part in range(parts):
        await_bytes(sent.at[: wide - 1, rows_of(part), :], send_sem.at[part])
    await_bytes(tell.at[: wide - 1], tell_sem.at[0])
    await_bytes(got, got_sem.at[0])
    for channel in range(chans):
        out_ref[:, channel, :] = got[channel].astype(jnp.float32)
    await_bytes(give.at[: wide - 1], give_sem.at[0])


def fused(voltages, taps, flags, positions, beam_index):
    wide = lax.axis_size("wide")
    count, _, length = voltages.shape
    ntaps, chans = taps.shape
    total = length // chans - ntaps + 1
    beams = beam_index.shape[0]
    hop = ROWS * chans
    window = -(-(ROWS + ntaps - 1) * chans // LANES) * LANES
    padded = (total // ROWS - 1) * hop + window
    bounds = [0, LANES // 2, total // 2, total]
    parts = len(bounds) - 1
    share = beams // wide
    width = wide * LANES
    vmem = pl.BlockSpec(memory_space=pltpu.VMEM)
    return pl.pallas_call(
        functools.partial(
            kernel, wide=wide, total=total, chans=chans, window=window, bounds=bounds,
            early=2,
        ),
        out_shape=jax.ShapeDtypeStruct((share, chans, total // 4), jnp.float32),
        in_specs=[pl.BlockSpec(memory_space=pl.ANY)] * 5,
        out_specs=vmem,
        scratch_shapes=[
            pltpu.VMEM(voltages.shape, jnp.bfloat16),
            pltpu.VMEM(taps.shape, jnp.float32),
            pltpu.VMEM((1, count), jnp.int32),
            pltpu.VMEM(positions.shape, jnp.float32),
            pltpu.VMEM((1, beams), jnp.int32),
            pltpu.VMEM((2 * hop, 2 * window), jnp.bfloat16),
            pltpu.VMEM((2 * LANES, padded), jnp.bfloat16),
            pltpu.VMEM((chans, total, LANES), jnp.bfloat16),
            pltpu.VMEM((wide, total, LANES), jnp.bfloat16),
            pltpu.VMEM((beams, width), jnp.float32),
            pltpu.VMEM((beams, width), jnp.float32),
            pltpu.VMEM((2 * beams, width), jnp.bfloat16),
            pltpu.VMEM((2 * beams, total), jnp.bfloat16),
            pltpu.VMEM((beams, width), jnp.float32),
            pltpu.VMEM((8, width), jnp.float32),
            pltpu.VMEM((chans, 8, LANES), jnp.float32),
            pltpu.VMEM((wide, 8, LANES), jnp.float32),
            pltpu.VMEM((wide, share, total // 4), jnp.bfloat16),
            pltpu.VMEM((chans, share, total // 4), jnp.bfloat16),
            pltpu.SemaphoreType.DMA((6,)),
            pltpu.SemaphoreType.DMA((parts,)),
            pltpu.SemaphoreType.DMA((parts,)),
            pltpu.SemaphoreType.DMA((1,)),
            pltpu.SemaphoreType.DMA((1,)),
            pltpu.SemaphoreType.DMA((1,)),
            pltpu.SemaphoreType.DMA((1,)),
        ],
        compiler_params=pltpu.CompilerParams(
            collective_id=0, has_side_effects=True, vmem_limit_bytes=64 * 2**20 - 2**16
        ),
    )(voltages, taps, flags.reshape(1, -1), positions, beam_index.reshape(1, -1))


def fits(voltages, taps, beam_index, wide):
    count, _, length = voltages.shape
    ntaps, chans = taps.shape
    total = length // chans - ntaps + 1
    return (
        2 * count == LANES
        and chans == wide
        and (ROWS * chans) % LANES == 0
        and wide % 2 == 0
        and total % 256 == 0
        and beam_index.shape[0] % (ROWS * wide) == 0
        and (total // 4) % LANES == 0
    )


def local(voltages, taps, flags, positions, beam_index):
    if fits(voltages, taps, beam_index, lax.axis_size("wide")):
        return fused(voltages, taps, flags, positions, beam_index)
    return plain(voltages, taps, flags, positions, beam_index)


def solution(mesh):
    in_specs = (P(("grp", "wide"), None, None), P(), P(("grp", "wide")), P(), P("grp"))
    out_specs = P(("grp", "wide"), None, None)
    return jax.shard_map(local, mesh=mesh, in_specs=in_specs, out_specs=out_specs, check_vma=False)
```

```python
import functools
import math

import jax
import jax.numpy as jnp
import numpy as np
from jax import lax
from jax.experimental import pallas as pl
from jax.experimental.pallas import tpu as pltpu
from jax.sharding import PartitionSpec as P

ITERS = 2


damping = 0.5
grid_side = 32


def channelize(voltages, taps, flags):
    count = voltages.shape[0]
    chans = taps.shape[1]
    ntaps = taps.shape[0]
    total = voltages.shape[2] // chans - ntaps + 1
    samples = voltages.astype(jnp.float32).reshape(count, 2, total + ntaps - 1, chans)
    filtered = taps[0][None, None, None, :] * samples[:, :, 0:total, :]
    for tap in range(1, ntaps):
        filtered = filtered + taps[tap][None, None, None, :] * samples[:, :, tap : tap + total, :]
    branch = jnp.arange(chans, dtype=jnp.int32)
    angle = 2.0 * math.pi / chans * (branch[:, None] * branch[None, :] % chans).astype(jnp.float32)
    cosine = jnp.cos(angle)
    sine = jnp.sin(angle)
    high = lax.Precision.HIGHEST
    real_in = filtered[:, 0]
    imag_in = filtered[:, 1]
    real_out = jnp.einsum("asp,pc->acs", real_in, cosine, precision=high) + jnp.einsum(
        "asp,pc->acs", imag_in, sine, precision=high
    )
    imag_out = jnp.einsum("asp,pc->acs", imag_in, cosine, precision=high) - jnp.einsum(
        "asp,pc->acs", real_in, sine, precision=high
    )
    keep = flags.astype(jnp.float32)[:, None, None] / math.sqrt(chans)
    return jnp.stack([real_out * keep, imag_out * keep]).astype(jnp.bfloat16)


def steering(channel, positions, beam_index, chans):
    column = (beam_index % grid_side).astype(jnp.float32)
    row_cell = (beam_index // grid_side).astype(jnp.float32)
    east = (column + 0.5) / grid_side - 0.5
    north = (row_cell + 0.5) / grid_side - 0.5
    ratio = 1.0 + 0.5 * channel.astype(jnp.float32) / chans
    phase = (
        2.0
        * math.pi
        * ratio
        * (positions[0][:, None] * east[None, :] + positions[1][:, None] * north[None, :])
    )
    return (jnp.cos(phase), -jnp.sin(phase))


def form_beams(blocks, channel, positions, beam_index, total, chans):
    high = lax.Precision.HIGHEST
    cov_real = 0.0
    cov_imag = 0.0
    for block in blocks:
        left = jnp.concatenate([block[0], block[1]], axis=1)
        turned = jnp.concatenate([block[1], -block[0]], axis=1)
        cov_real = cov_real + jnp.dot(left, left.T, preferred_element_type=jnp.float32)
        cov_imag = cov_imag + jnp.dot(turned, left.T, preferred_element_type=jnp.float32)
    cov_real = cov_real / total
    cov_imag = cov_imag / total
    count = cov_real.shape[0]
    diagonal = jnp.diagonal(cov_real)
    loading = jnp.mean(diagonal) + 1e-05
    scaling = (damping / (diagonal + loading))[:, None]
    steer_real, steer_imag = steering(channel, positions, beam_index, chans)
    weight_real = scaling * steer_real
    weight_imag = scaling * steer_imag
    for sweep in range(ITERS):
        image_real = (
            jnp.dot(cov_real, weight_real, precision=high)
            - jnp.dot(cov_imag, weight_imag, precision=high)
            + loading * weight_real
        )
        image_imag = (
            jnp.dot(cov_real, weight_imag, precision=high)
            + jnp.dot(cov_imag, weight_real, precision=high)
            + loading * weight_imag
        )
        weight_real = weight_real + scaling * (steer_real - image_real)
        weight_imag = weight_imag + scaling * (steer_imag - image_imag)
    low_real = weight_real.astype(jnp.bfloat16)
    low_imag = weight_imag.astype(jnp.bfloat16)
    plain = jnp.concatenate([low_real, low_imag], axis=0)
    mixed = jnp.concatenate([low_real, -low_imag], axis=0)
    contract = (((0,), (0,)), ((), ()))
    reals = []
    imags = []
    for block in blocks:
        reals.append(
            lax.dot_general(
                plain,
                jnp.concatenate([block[0], block[1]], axis=0),
                contract,
                preferred_element_type=jnp.float32,
            )
        )
        imags.append(
            lax.dot_general(
                mixed,
                jnp.concatenate([block[1], block[0]], axis=0),
                contract,
                preferred_element_type=jnp.float32,
            )
        )
    norm_factor = 1.0 / math.sqrt(count)
    beams = (
        jnp.stack([jnp.concatenate(reals, axis=-1), jnp.concatenate(imags, axis=-1)]) * norm_factor
    )
    return beams.astype(jnp.bfloat16)


def detect(beams):
    floats = beams.astype(jnp.float32)
    energy = floats[:, 0] * floats[:, 0] + floats[:, 1] * floats[:, 1]
    shape = energy.shape
    return energy.reshape(shape[0], shape[1], shape[2] // 4, 4).sum(axis=-1)


def plain(voltages, taps, flags, positions, beam_index):
    spectra = channelize(voltages, taps, flags)
    chans = taps.shape[1]
    per_dev = chans // lax.axis_size("wide")
    first = lax.axis_index("wide") * per_dev
    total = spectra.shape[3]
    pieces = [lax.all_to_all(spectra, "wide", split_axis=2, concat_axis=1, tiled=True)]
    stacked = [jnp.moveaxis(piece, 2, 0) for piece in pieces]

    def one_channel(operands):
        offset, blocks = operands
        return form_beams(blocks, first + offset, positions, beam_index, total, chans)

    beams = lax.map(one_channel, (jnp.arange(per_dev, dtype=jnp.int32), stacked))
    result = lax.all_to_all(
        detect(beams).astype(jnp.bfloat16), "wide", split_axis=1, concat_axis=0, tiled=True
    ).astype(jnp.float32)
    return jnp.transpose(result, (1, 0, 2))


MESH = pl.DeviceIdType.MESH
LANES = 128
ROWS = 16
NT = (((1,), (1,)), ((), ()))


def cosine_turns(turns):
    frac = jnp.abs(turns - jnp.floor(turns + 0.5))
    x = (0.25 - frac) * (2.0 * math.pi)
    sq = x * x
    poly = -1.0 / 39916800.0
    for term in (1.0 / 362880.0, -1.0 / 5040.0, 1.0 / 120.0, -1.0 / 6.0, 1.0):
        poly = poly * sq + term
    return x * poly


def swap_halves(block):
    return pltpu.roll(block, LANES // 2, 1)


def kernel(
    volt_hbm, taps_hbm, flags_hbm, place_hbm, index_hbm, out_ref,
    volt, taps_ref, flags_ref, place_ref, index_ref, bank, mixed, sent, spec, steer, weight, low, image, applied, scale,
    tell, told, give, got,
    volt_sem, send_sem, recv_sem, tell_sem, told_sem, give_sem, got_sem,
    *, wide, total, chans, window, bounds, early,
):
    me = lax.axis_index("wide")
    parts = len(bounds) - 1
    beams = index_hbm.shape[1]
    width = wide * LANES
    hop = ROWS * chans
    length = volt_hbm.shape[2]
    ntaps = taps_hbm.shape[0]
    half_lanes = LANES // 2

    barrier = pltpu.get_barrier_semaphore()
    first_reach = bounds[1] * chans + window - hop
    loads = [
        pltpu.make_async_copy(source, target, volt_sem.at[at])
        for at, (source, target) in enumerate(
            [
                (taps_hbm, taps_ref),
                (flags_hbm, flags_ref),
                (place_hbm, place_ref),
                (index_hbm, index_ref),
                (volt_hbm.at[:, :, :first_reach], volt.at[:, :, :first_reach]),
                (volt_hbm.at[:, :, first_reach:], volt.at[:, :, first_reach:]),
            ]
        )
    ]
    for load in loads:
        load.start()

    def greet(off, carry):
        pl.semaphore_signal(
            barrier, inc=1, device_id={"wide": lax.rem(me + off, wide)}, device_id_type=MESH
        )
        return carry

    lax.fori_loop(1, wide, greet, 0)

    ranked = sorted(range(1, wide), key=lambda off: (abs(off - wide // 2), off))
    cut = (len(ranked) + 1) // 2
    mixed_order = [
        entry for duo in zip(ranked[:cut], ranked[cut:] + [None]) for entry in duo
    ]
    mixed_order = [entry for entry in mixed_order if entry is not None]
    turned_order = list(mixed_order)
    for at in range(0, len(turned_order) - 1, 2):
        turned_order[at], turned_order[at + 1] = turned_order[at + 1], turned_order[at]

    def everyone(act):
        core = lax.rem(me, 2)
        for one, two in zip(mixed_order, turned_order):
            act(lax.rem(me + (one + core * (two - one)), wide))

    def iota(shape, axis):
        return lax.broadcasted_iota(jnp.int32, shape, axis)

    for load in loads[:4]:
        load.wait()
    slot = iota((ROWS, window), 1) // chans
    delay = slot - iota((ROWS, window), 0)
    spread = jnp.where(iota((chans, window), 1) % chans == iota((chans, window), 0), 1.0, 0.0)
    tiled = jnp.dot(
        taps_ref[...], spread, precision=lax.Precision.HIGHEST, preferred_element_type=jnp.float32
    )
    filt = jnp.zeros((ROWS, window), jnp.float32)
    for tap in range(ntaps):
        filt = filt + jnp.where(delay == tap, tiled[tap : tap + 1, :], 0.0)
    spin = (iota((chans, window), 0) * (iota((chans, window), 1) % chans)) % chans
    spin = spin.astype(jnp.float32) / chans
    for half in range(2):
        wave = cosine_turns(spin - 0.25 * half) / math.sqrt(chans)
        for channel in range(chans):
            entry = wave[channel : channel + 1, :] * filt
            top = entry.astype(jnp.bfloat16)
            rest = (entry - top.astype(jnp.float32)).astype(jnp.bfloat16)
            cols = slice(half * window, (half + 1) * window)
            bank[channel * ROWS : (channel + 1) * ROWS, cols] = top
            bank[hop + channel * ROWS : hop + (channel + 1) * ROWS, cols] = rest

    doubled = jnp.where(iota((half_lanes, LANES), 1) // 2 == iota((half_lanes, LANES), 0), 1.0, 0.0)
    keep = jnp.broadcast_to(flags_ref[...].astype(jnp.float32), (8, half_lanes))
    keep = jnp.dot(
        keep.astype(jnp.bfloat16), doubled.astype(jnp.bfloat16), preferred_element_type=jnp.float32
    )[0:1]
    row = iota((2 * LANES, LANES), 0)
    antenna = row % half_lanes
    quarter = row // half_lanes
    from_part = jnp.where((quarter == 1) | (quarter == 2), 1, 0)
    chosen = iota((2 * LANES, LANES), 1) == 2 * antenna + from_part
    order = jnp.where(chosen, jnp.where(quarter == 3, -keep, keep), 0.0).astype(jnp.bfloat16)

    def mix(start, size):
        block = volt[:, :, start : start + size].reshape(LANES, size)
        mixed[:, start : start + size] = jnp.dot(
            order, block, preferred_element_type=jnp.float32
        ).astype(jnp.bfloat16)

    def rows_of(part):
        return slice(bounds[part], bounds[part + 1])

    def lanes_of(block):
        return pl.ds(pl.multiple_of(block * LANES, LANES), LANES)

    def remote(source, target, out_sem, in_sem, other):
        return pltpu.make_async_remote_copy(
            src_ref=source,
            dst_ref=target,
            send_sem=out_sem,
            recv_sem=in_sem,
            device_id={"wide": other},
            device_id_type=MESH,
        )

    def await_bytes(ref, sem):
        pltpu.make_async_copy(ref, ref, sem).wait()

    def ship(part):
        rows = rows_of(part)
        everyone(
            lambda other: remote(
                sent.at[other, rows, :], spec.at[me, rows, :],
                send_sem.at[part], recv_sem.at[part], other,
            ).start()
        )
        pltpu.make_async_copy(
            sent.at[me, rows, :], spec.at[me, rows, :], recv_sem.at[part]
        ).start()

    tell[...] = jnp.zeros_like(tell)

    def channelize_pair(pair, carry):
        start = pl.multiple_of(pair * (2 * hop), LANES)
        acc = jnp.zeros((hop, 2 * LANES), jnp.float32)
        for half in range(2):
            rows = slice(half * LANES, (half + 1) * LANES)
            cols = slice(half * window, (half + 1) * window)
            both = jnp.concatenate(
                [
                    mixed[rows, pl.ds(start, window)],
                    mixed[rows, pl.ds(pl.multiple_of(start + hop, LANES), window)],
                ],
                axis=0,
            )
            for piece in range(2):
                acc = acc + lax.dot_general(
                    bank[piece * hop : (piece + 1) * hop, cols], both, NT,
                    preferred_element_type=jnp.float32,
                )
        rounded = acc.astype(jnp.bfloat16)
        for side in range(2):
            at = pl.multiple_of(pair * (2 * ROWS) + side * ROWS, ROWS)
            block = rounded[:, side * LANES : (side + 1) * LANES].reshape(chans, ROWS, LANES)
            sent[:, pl.ds(at, ROWS), :] = block
            block = block.astype(jnp.float32)
            block = block * block
            tell[...] += block[:, :8] + block[:, 8:]
        return carry

    loads[4].wait()
    tail = length // LANES * LANES
    mixed[:, tail:] = jnp.zeros((2 * LANES, mixed.shape[1] - tail), jnp.bfloat16)
    over = window - hop
    reach = 0
    for part in range(parts):
        if part == 1:
            loads[5].wait()
        upto = min(bounds[part + 1] * chans + over, length)
        mix(reach, upto - reach)
        reach = upto
        span = 2 * ROWS
        lax.fori_loop(bounds[part] // span, bounds[part + 1] // span, channelize_pair, 0)
        if part == 0:
            pl.semaphore_wait(barrier, wide - 1)
        if part < early:
            ship(part)
    everyone(
        lambda other: remote(
            tell.at[other], told.at[me], tell_sem.at[0], told_sem.at[0], other
        ).start()
    )
    pltpu.make_async_copy(tell.at[me], told.at[me], told_sem.at[0]).start()
    for part in range(early, parts):
        ship(part)

    index = index_ref[...]
    ratio = 1.0 + 0.5 * me.astype(jnp.float32) / chans
    cells = [
        ((index % grid_side).astype(jnp.float32) + 0.5) / grid_side - 0.5,
        ((index // grid_side).astype(jnp.float32) + 0.5) / grid_side - 0.5,
    ]
    same = iota((beams, beams), 0) == iota((beams, beams), 1)
    east, north = [
        jnp.sum(jnp.where(same, cell, 0.0), axis=1, keepdims=True) * ratio for cell in cells
    ]
    first_half = iota((1, LANES), 1) < half_lanes
    turn = jnp.where(first_half, 0.0, 0.25)

    def steer_duo(duo, carry):
        here = place_ref[:, lanes_of(duo)]
        here = jnp.concatenate([here, jnp.zeros((6, LANES), jnp.float32)], axis=0)
        there = swap_halves(here)
        for side in range(2):
            both = jnp.where(first_half, here, there) if side == 0 else jnp.where(
                first_half, there, here
            )
            turns = east * both[0:1] + north * both[1:2] + turn
            steer[:, lanes_of(2 * duo + side)] = cosine_turns(turns)
        return carry

    lax.fori_loop(0, wide // 2, steer_duo, 0)

    await_bytes(told, told_sem.at[0])
    sign = jnp.where(first_half, 1.0, -1.0)
    power = jnp.sum(told[...], axis=1, keepdims=True) * (1.0 / total)
    loading = jnp.sum(power) / (width // 2) + 1e-05
    for block in range(wide):
        piece = jnp.broadcast_to(power[block], (8, LANES))
        piece = piece + swap_halves(piece)
        scale[:, block * LANES : (block + 1) * LANES] = 0.5 / (piece + loading)

    def keep_low(lanes, value):
        low[:beams, lanes] = value.astype(jnp.bfloat16)
        low[beams:, lanes] = (swap_halves(value) * sign).astype(jnp.bfloat16)

    def first_block(block, carry):
        lanes = lanes_of(block)
        value = scale[0:1, lanes] * steer[:, lanes]
        weight[:, lanes] = value
        keep_low(lanes, value)
        return carry

    lax.fori_loop(0, wide, first_block, 0)

    def project(rows):
        strip = jnp.concatenate([spec[block, rows, :] for block in range(wide)], axis=1)
        return lax.dot_general(low[...], strip, NT, preferred_element_type=jnp.float32)

    def back_project(rows, last, sweep, first):
        def duo_block(duo, carry):
            strip = jnp.concatenate([spec[2 * duo, rows, :], spec[2 * duo + 1, rows, :]], axis=1)
            back = jnp.dot(image[:, rows], strip, preferred_element_type=jnp.float32)
            for side in range(2):
                lanes = lanes_of(2 * duo + side)
                cols = slice(side * LANES, (side + 1) * LANES)
                fresh = back[:beams, cols] - sign * swap_halves(back[beams:, cols])
                if not first:
                    fresh = applied[:, lanes] + fresh
                if not last:
                    applied[:, lanes] = fresh
                    continue
                value = weight[:, lanes]
                value = value + scale[0:1, lanes] * (
                    steer[:, lanes] - (fresh * (1.0 / total) + loading * value)
                )
                if sweep < ITERS - 1:
                    weight[:, lanes] = value
                keep_low(lanes, value)
            return carry

        lax.fori_loop(0, wide // 2, duo_block, 0)

    for part in range(parts):
        rows = rows_of(part)
        await_bytes(spec.at[:, rows, :], recv_sem.at[part])
        if bounds[part + 1] % (total // 2):
            continue
        rows = slice(bounds[part + 1] - total // 2, bounds[part + 1])
        image[:, rows] = project(rows).astype(jnp.bfloat16)
        back_project(rows, part + 1 == parts, 0, rows.start == 0)

    half_rows = total // 2
    halves = [slice(half * half_rows, (half + 1) * half_rows) for half in range(2)]
    for sweep in range(1, ITERS):
        for rows in halves:
            image[:, rows] = project(rows).astype(jnp.bfloat16)
        back_project(slice(0, total), True, sweep, True)

    group = total // 4
    share = give.shape[1]
    sums = jnp.zeros((beams, group), jnp.float32)
    for half, rows in enumerate(halves):
        value = project(rows)
        energy = value[:beams] * value[:beams] + value[beams:] * value[beams:]
        energy = energy * (2.0 / width)
        top = energy.astype(jnp.bfloat16)
        rest = (energy - top.astype(jnp.float32)).astype(jnp.bfloat16)
        source = iota((half_rows, group), 0) + half * half_rows
        target = iota((half_rows, group), 1) * 4
        pick = jnp.where((source >= target) & (source < target + 4), 1.0, 0.0)
        pick = pick.astype(jnp.bfloat16)
        sums = sums + jnp.dot(top, pick, preferred_element_type=jnp.float32)
        sums = sums + jnp.dot(rest, pick, preferred_element_type=jnp.float32)
    give[...] = sums.astype(jnp.bfloat16).reshape(wide, share, group)
    everyone(
        lambda other: remote(
            give.at[other], got.at[me], give_sem.at[0], got_sem.at[0], other
        ).start()
    )
    pltpu.make_async_copy(give.at[me], got.at[me], got_sem.at[0]).start()
    for part in range(parts):
        await_bytes(sent.at[: wide - 1, rows_of(part), :], send_sem.at[part])
    await_bytes(tell.at[: wide - 1], tell_sem.at[0])
    await_bytes(got, got_sem.at[0])
    for channel in range(chans):
        out_ref[:, channel, :] = got[channel].astype(jnp.float32)
    await_bytes(give.at[: wide - 1], give_sem.at[0])


def fused(voltages, taps, flags, positions, beam_index):
    wide = lax.axis_size("wide")
    count, _, length = voltages.shape
    ntaps, chans = taps.shape
    total = length // chans - ntaps + 1
    beams = beam_index.shape[0]
    hop = ROWS * chans
    window = -(-(ROWS + ntaps - 1) * chans // LANES) * LANES
    padded = (total // ROWS - 1) * hop + window
    bounds = [0, total // 8, total // 4, total // 2, 3 * total // 4, 7 * total // 8, total]
    parts = len(bounds) - 1
    share = beams // wide
    width = wide * LANES
    vmem = pl.BlockSpec(memory_space=pltpu.VMEM)
    return pl.pallas_call(
        functools.partial(
            kernel, wide=wide, total=total, chans=chans, window=window, bounds=bounds,
            early=parts - 1,
        ),
        out_shape=jax.ShapeDtypeStruct((share, chans, total // 4), jnp.float32),
        in_specs=[pl.BlockSpec(memory_space=pl.ANY)] * 5,
        out_specs=vmem,
        scratch_shapes=[
            pltpu.VMEM(voltages.shape, jnp.bfloat16),
            pltpu.VMEM(taps.shape, jnp.float32),
            pltpu.VMEM((1, count), jnp.int32),
            pltpu.VMEM(positions.shape, jnp.float32),
            pltpu.VMEM((1, beams), jnp.int32),
            pltpu.VMEM((2 * hop, 2 * window), jnp.bfloat16),
            pltpu.VMEM((2 * LANES, padded), jnp.bfloat16),
            pltpu.VMEM((chans, total, LANES), jnp.bfloat16),
            pltpu.VMEM((wide, total, LANES), jnp.bfloat16),
            pltpu.VMEM((beams, width), jnp.float32),
            pltpu.VMEM((beams, width), jnp.float32),
            pltpu.VMEM((2 * beams, width), jnp.bfloat16),
            pltpu.VMEM((2 * beams, total), jnp.bfloat16),
            pltpu.VMEM((beams, width), jnp.float32),
            pltpu.VMEM((8, width), jnp.float32),
            pltpu.VMEM((chans, 8, LANES), jnp.float32),
            pltpu.VMEM((wide, 8, LANES), jnp.float32),
            pltpu.VMEM((wide, share, total // 4), jnp.bfloat16),
            pltpu.VMEM((chans, share, total // 4), jnp.bfloat16),
            pltpu.SemaphoreType.DMA((6,)),
            pltpu.SemaphoreType.DMA((parts,)),
            pltpu.SemaphoreType.DMA((parts,)),
            pltpu.SemaphoreType.DMA((1,)),
            pltpu.SemaphoreType.DMA((1,)),
            pltpu.SemaphoreType.DMA((1,)),
            pltpu.SemaphoreType.DMA((1,)),
        ],
        compiler_params=pltpu.CompilerParams(
            collective_id=0, has_side_effects=True, vmem_limit_bytes=64 * 2**20 - 2**16
        ),
    )(voltages, taps, flags.reshape(1, -1), positions, beam_index.reshape(1, -1))


def fits(voltages, taps, beam_index, wide):
    count, _, length = voltages.shape
    ntaps, chans = taps.shape
    total = length // chans - ntaps + 1
    return (
        2 * count == LANES
        and chans == wide
        and (ROWS * chans) % LANES == 0
        and wide % 2 == 0
        and total % 256 == 0
        and beam_index.shape[0] % (ROWS * wide) == 0
        and (total // 4) % LANES == 0
    )


def local(voltages, taps, flags, positions, beam_index):
    if fits(voltages, taps, beam_index, lax.axis_size("wide")):
        return fused(voltages, taps, flags, positions, beam_index)
    return plain(voltages, taps, flags, positions, beam_index)


def solution(mesh):
    in_specs = (P(("grp", "wide"), None, None), P(), P(("grp", "wide")), P(), P("grp"))
    out_specs = P(("grp", "wide"), None, None)
    return jax.shard_map(local, mesh=mesh, in_specs=in_specs, out_specs=out_specs, check_vma=False)
```
